32 devices in a mesh: dp: 4 (over y, core), dom: 8 (over z, x).
Axes of the slice: x: 2, y: 2, z: 4, core: 2. Of those that a mesh axis runs over, the one named last changes fastest.
Arguments:
- features: bfloat16 [32768, 1024], P(('dp', 'dom')), may hold values from -6 to 6
- w_first: bfloat16 [1024, 1024], replicated, may hold values from -0.1875 to 0.1875
- b_first: bfloat16 [1024], replicated, may hold values from -3 to 3
- w_second: bfloat16 [1024, 256], replicated, may hold values from -0.1875 to 0.1875
- b_second: bfloat16 [256], replicated, may hold values from -3 to 3
- dest_part: int32 [32768], P(('dp', 'dom')), may hold values from 0 to 31, as said below
- dest_slot: int32 [32768], P(('dp', 'dom')), may hold values from 0 to 3071, as said below
- tile_coords: int32 [1536, 2], P(('dp', 'dom')), may hold values from 0 to 39, as said below
- tile_values: bfloat16 [1536, 128, 128], P(('dp', 'dom')), may hold values from -0.25 to 0.25
- halo_send: int32 [32, 2, 8], P(('dp', 'dom')), may hold values from 0 to 23, as said below
Outputs:
- smoothed: bfloat16 [98304, 256], P(('dp', 'dom'))
The draws below stay inside these ranges and needn't reach their ends.
Inputs may be any that keep to these rules, and one draw needn't show every extreme that they name: `dest_part`: every part holds at most 3072 rows and one part exactly 3072; the rows of one part are dealt over the devices so that the counts that two devices send it differ by at most one, so at most 96 rows go from one device to one part and every device sends exactly 96 to the fullest part. `dest_slot`: within a part, its rows take the slots 0 to its size minus one, each once. `tile_coords`: 48 tiles a part, parts in order. Column 0 is a block of the part; column 1 indexes its extended blocks. The part's first 24 tiles are (b, b) for each block b, the next 16 have sources 24 to 39 in order. `halo_send`: listed blocks hold rows of the part and may repeat.
All inputs are finite; a program needn't handle non-finite values.
Results may differ from the reference program's by a relative error of at most 0.0062.
Values may be sent and summed in bfloat16 or wider, within the bound.
No kernel may reach another device: no remote copies, remote signals or barrier semaphores. Data moves between devices by JAX's collectives and lax.ppermute only.
A program may use at most 64 MiB of HBM per device.

```python
import jax
import jax.numpy as jnp
from jax import lax

D_IN = 1024
HID = 1024
D = 256
BLK = 128
HOPS = 2
HB = 8
R_DEV = 1024
PARTS_SIZE = 32
ROWS = 32768
CAP = 3072
NB = 24
TILES_DEV = 48
N_DP = 4
N_DOM = 8


def dealing(key):
    keys = jax.random.split(key, 4)
    part_ids = jnp.arange(PARTS_SIZE, dtype=jnp.int32)
    fullest = jax.random.randint(keys[0], (), 0, PARTS_SIZE)
    weights = jax.random.randint(keys[1], (PARTS_SIZE,), 2, 6)
    weights = jnp.where(part_ids == fullest, 0, weights)
    remainder = (PARTS_SIZE - 3) * R_DEV
    sizes = weights * remainder // jnp.sum(weights)
    leftover = remainder - jnp.sum(sizes)
    ranking = part_ids - (part_ids > fullest).astype(jnp.int32)
    sizes = sizes + jnp.where((part_ids != fullest) & (ranking < leftover), 1, 0)
    sizes = jnp.where(part_ids == fullest, CAP, sizes).astype(jnp.int32)
    ends = jnp.cumsum(sizes).astype(jnp.int32)
    starts = ends - sizes
    entries = jnp.arange(PARTS_SIZE * R_DEV, dtype=jnp.int32)
    owner = jnp.searchsorted(ends, entries, side='right').astype(jnp.int32)
    shuffled = jax.random.permutation(keys[2], PARTS_SIZE * R_DEV).astype(jnp.int32)
    grouped = shuffled[jnp.argsort(owner[shuffled], stable=True)]
    slot_of = grouped - starts[owner]
    combined = owner * CAP + slot_of
    dealt = combined.reshape(R_DEV, PARTS_SIZE).T
    dealt = jax.random.permutation(keys[3], dealt, axis=1, independent=True)
    return (dealt.reshape(PARTS_SIZE * R_DEV).astype(jnp.int32), sizes)


def draw_dest_part(key, part):
    dealt, sizes = dealing(key)
    return (dealt // CAP).astype(jnp.int32)


def draw_dest_slot(key, part):
    dealt, sizes = dealing(key)
    return (dealt % CAP).astype(jnp.int32)


def draw_tile_coords(key, part):
    dealt, sizes = dealing(key)
    key = jax.random.fold_in(key, 3)
    keys = jax.random.split(key, 2)
    live = ((sizes + BLK - 1) // BLK)[:, None]
    extra = TILES_DEV - NB
    raw_dest = jax.random.randint(keys[0], (PARTS_SIZE, extra), 0, 1 << 20)
    dest_rest = raw_dest % live
    raw_source = jax.random.randint(keys[1], (PARTS_SIZE, extra - 2 * HB), 0, 1 << 20)
    pick = raw_source % (live + 2 * HB)
    source_rest = jnp.where(pick < live, pick, NB + pick - live)
    diagonal = jnp.broadcast_to(jnp.arange(NB, dtype=jnp.int32)[None, :], (PARTS_SIZE, NB))
    halo_source = jnp.broadcast_to(NB + jnp.arange(2 * HB, dtype=jnp.int32)[None, :], (PARTS_SIZE, 2 * HB))
    dest_all = jnp.concatenate([diagonal, dest_rest.astype(jnp.int32)], axis=1)
    source_all = jnp.concatenate([diagonal, halo_source, source_rest.astype(jnp.int32)], axis=1)
    return jnp.stack([dest_all, source_all], axis=-1).reshape(PARTS_SIZE * TILES_DEV, 2).astype(jnp.int32)


def draw_halo_send(key, part):
    dealt, sizes = dealing(key)
    key = jax.random.fold_in(key, 4)
    live = ((sizes + BLK - 1) // BLK)[:, None, None]
    raw_blocks = jax.random.randint(key, (PARTS_SIZE, 2, HB), 0, 1 << 20)
    blocks = raw_blocks % live
    fullest_part = (sizes == CAP)[:, None, None]
    entry_a = jnp.arange(2, dtype=jnp.int32)[None, :, None] == 0
    entry_b = jnp.arange(HB, dtype=jnp.int32)[None, None, :] == HB - 1
    blocks = jnp.where(fullest_part & entry_a & entry_b, NB - 1, blocks)
    return blocks.astype(jnp.int32)


def block_levels(key, shape, pieces, smallest, high):
    gain = 1.0
    for dim, blocks in pieces:
        heights = jax.random.uniform(jax.random.fold_in(jax.random.fold_in(key, 6), dim), (blocks,), jnp.float32, smallest / len(pieces), high / len(pieces))
        gain = gain * jnp.repeat(jnp.exp(heights), shape[dim] // blocks).reshape((-1,) + (1,) * (len(shape) - 1 - dim))
    return gain


def scatter_about(stream_key, shape, spread, most, cuts=(), held_as=jnp.bfloat16):
    result = jax.random.normal(stream_key, shape, jnp.float32) * spread
    if len(cuts) > 0:
        result = block_levels(stream_key, shape, cuts, -0.22, 0.18) * result
    return jnp.clip(result, min=-most, max=most).astype(held_as)


def setup_inputs(seed: int = 0) -> dict:
    arg_keys = jax.random.split(jax.random.key(seed), 11)
    features = scatter_about(arg_keys[0], (ROWS, D_IN), 1.0, 6.0, ((0, 32),))
    w_first = scatter_about(arg_keys[1], (D_IN, HID), D_IN ** -0.5, 0.1875)
    b_first = scatter_about(arg_keys[2], (HID,), 0.5, 3.0)
    w_second = scatter_about(arg_keys[3], (HID, D), HID ** -0.5, 0.1875)
    b_second = scatter_about(arg_keys[4], (D,), 0.5, 3.0)
    dest_part = draw_dest_part(jax.random.fold_in(arg_keys[10], 71), 0)
    dest_slot = draw_dest_slot(jax.random.fold_in(arg_keys[10], 71), 0)
    tile_coords = draw_tile_coords(jax.random.fold_in(arg_keys[10], 71), 0)
    tile_values = scatter_about(arg_keys[8], (PARTS_SIZE * TILES_DEV, BLK, BLK), 0.045, 0.25, ((0, 32),))
    halo_send = draw_halo_send(jax.random.fold_in(arg_keys[10], 71), 0)
    return {"features": features, "w_first": w_first, "b_first": b_first, "w_second": w_second, "b_second": b_second, "dest_part": dest_part, "dest_slot": dest_slot, "tile_coords": tile_coords, "tile_values": tile_values, "halo_send": halo_send}


ALPHA = 0.1


def project(piece, w_first, b_first, w_second, b_second):
    hidden = jnp.dot(piece, w_first, preferred_element_type=jnp.float32) + b_first.astype(jnp.float32)
    hidden = jax.nn.gelu(hidden, approximate=False).astype(jnp.bfloat16)
    output = jnp.dot(hidden, w_second, preferred_element_type=jnp.float32) + b_second.astype(jnp.float32)
    return output.astype(jnp.bfloat16)


def merged_parts(array):
    return array.reshape((N_DP * N_DOM,) + array.shape[2:])


def one_part(items):
    own, low_blocks, low_list, up_blocks, up_list, coord, value, anchor, occupied = items
    extended = jnp.concatenate([own, low_blocks[low_list], up_blocks[up_list]], axis=0)
    picked = extended[coord[:, 1]].astype(jnp.float32)
    contrib = jnp.einsum("tij,tjd->tid", value.astype(jnp.float32), picked)
    summed = jax.ops.segment_sum(contrib, coord[:, 0], num_segments=NB).reshape(CAP, D)
    mixed = (1.0 - ALPHA) * summed + ALPHA * anchor.astype(jnp.float32)
    return (occupied[:, None] * mixed).astype(jnp.bfloat16)


def reference(features, w_first, b_first, w_second, b_second, dest_part, dest_slot, tile_coords, tile_values, halo_send):
    part_count = N_DP * N_DOM
    embedded = lax.map(lambda piece: project(piece, w_first, b_first, w_second, b_second),
                       features.reshape(part_count, R_DEV, D_IN)).reshape(part_count * R_DEV, D)
    target = (dest_part * CAP + dest_slot).astype(jnp.int32)
    start = jnp.zeros((part_count * CAP, D), jnp.bfloat16).at[target].set(embedded)
    occupied = jnp.zeros((part_count * CAP,), jnp.float32).at[target].set(1.0)
    start = start.reshape(N_DP, N_DOM, CAP, D)
    occupied = occupied.reshape(N_DP, N_DOM, CAP)
    lists = halo_send.reshape(N_DP, N_DOM, 2, HB)
    coords = tile_coords.reshape(N_DP, N_DOM, TILES_DEV, 2)
    values = tile_values.reshape(N_DP, N_DOM, TILES_DEV, BLK, BLK)
    lower_lists = jnp.roll(lists[:, :, 0], 1, axis=1)
    upper_lists = jnp.roll(lists[:, :, 1], -1, axis=1)
    current = start
    for repeat in range(HOPS):
        blocks = current.reshape(N_DP, N_DOM, NB, BLK, D)
        lower = jnp.roll(blocks, 1, axis=1)
        upper = jnp.roll(blocks, -1, axis=1)
        items = (merged_parts(blocks), merged_parts(lower), merged_parts(lower_lists),
                 merged_parts(upper), merged_parts(upper_lists), merged_parts(coords),
                 merged_parts(values), merged_parts(start), merged_parts(occupied))
        current = lax.map(one_part, items).reshape(N_DP, N_DOM, CAP, D)
    return current.reshape(part_count * CAP, D)
```

```python
import functools

import jax
import jax.numpy as jnp
from jax import lax
from jax.experimental import pallas as pl
from jax.experimental.pallas import tpu as pltpu
from jax.sharding import PartitionSpec as P

HOPS = 2
ALPHA = 0.1
LANES = 128
PACK = 16
GROUP = LANES // PACK
VMEM_LIMIT = 48 * 1024 * 1024

BF16 = jnp.bfloat16
F32 = jnp.float32


def iota(shape, dim):
    return lax.broadcasted_iota(jnp.int32, shape, dim)


def gelu(value):
    return 0.5 * value * (1.0 + lax.erf(value * (0.5**0.5)))


def project_kernel(
    parts,
    slots,
    features,
    w_first,
    b_first,
    w_second,
    b_second,
    dest_part,
    dest_slot,
    lane_base,
    out,
    embedded,
):
    step = pl.program_id(0)
    block = features.shape[0]
    width = w_second.shape[1]
    total = None
    chunk = 256
    for first in range(0, w_first.shape[1], chunk):
        columns = slice(first, first + chunk)
        hidden = jnp.dot(features[...], w_first[:, columns], preferred_element_type=F32)
        hidden = gelu(hidden + b_first[:, columns].astype(F32)).astype(BF16)
        term = jnp.dot(hidden, w_second[columns, :], preferred_element_type=F32)
        total = term if total is None else total + term
    rows = pl.ds(pl.multiple_of(step * block, block), block)
    embedded[rows, :] = (total + b_second[...].astype(F32)).astype(BF16)

    @pl.when(step == pl.num_programs(0) - 1)
    def _():
        count = dest_part.shape[1]
        part = dest_part[...]
        onehot = (iota((parts, count), 0) == part).astype(F32)
        blocks = [onehot[:, at : at + LANES] for at in range(0, count, LANES)]
        earlier = (iota((LANES, LANES), 0) < iota((LANES, LANES), 1)).astype(BF16)
        within = jnp.dot(
            jnp.concatenate(blocks, axis=0).astype(BF16), earlier, preferred_element_type=F32
        )
        offset = jnp.zeros((parts, 1), F32)
        pieces = []
        for index, piece in enumerate(blocks):
            before = within[index * parts : (index + 1) * parts, :] + offset
            pieces.append(jnp.sum(before * piece, axis=0, keepdims=True))
            offset = offset + jnp.sum(piece, axis=1, keepdims=True)
        position = jnp.concatenate(pieces, axis=1).astype(jnp.int32)
        target = part * slots + position

        coded = dest_slot[...] + 1
        high = jnp.right_shift(coded, 6)
        low = coded - high * 64
        place = (iota((LANES, count), 0) == position).astype(BF16)
        digits = []
        for digit in (high, low):
            marked = (onehot * digit.astype(F32)).astype(BF16)
            digits.append(
                lax.dot_general(
                    marked, place, (((1,), (1,)), ((), ())), preferred_element_type=F32
                )
            )
        base = lane_base[0]
        lane = iota((parts, LANES), 1)
        mine = (lane >= base) & (lane < base + PACK)
        row = iota((parts, PACK, LANES), 1)
        listed = jnp.zeros((parts, PACK, LANES), F32)
        for at, digit in zip((0, 8), digits):
            for j in range(slots // PACK):
                turned = pltpu.roll(digit, lax.rem(base - j * PACK + LANES, LANES), 1)
                turned = jnp.where(mine, turned, 0.0)
                listed = jnp.where(row == at + j, turned[:, None, :], listed)
        halves = width // LANES
        out[:, halves * slots :, :] = listed.astype(BF16)

        size = GROUP * slots
        slot = iota((size, count), 0)
        for group in range(parts // GROUP):
            select = (slot == target - group * size).astype(BF16)
            moved = jnp.dot(select, embedded[...], preferred_element_type=F32).astype(BF16)
            for half in range(halves):
                piece = moved[:, half * LANES : (half + 1) * LANES]
                out[group * GROUP : (group + 1) * GROUP, half * slots : (half + 1) * slots, :] = (
                    piece.reshape(GROUP, slots, LANES)
                )


def project(parts, slots, features, w_first, b_first, w_second, b_second, part, slot, lane_base):
    rows, depth = features.shape
    hidden, width = w_second.shape
    block = rows // 4
    length = (width // LANES) * slots + PACK
    whole = lambda shape: pl.BlockSpec(shape, lambda i: (0,) * len(shape))
    return pl.pallas_call(
        functools.partial(project_kernel, parts, slots),
        out_shape=jax.ShapeDtypeStruct((parts, length, LANES), BF16),
        grid=(rows // block,),
        in_specs=[
            pl.BlockSpec((block, depth), lambda i: (i, 0)),
            whole((depth, hidden)),
            whole((1, hidden)),
            whole((hidden, width)),
            whole((1, width)),
            whole((1, rows)),
            whole((1, rows)),
            pl.BlockSpec(memory_space=pltpu.SMEM),
        ],
        out_specs=whole((parts, length, LANES)),
        scratch_shapes=[pltpu.VMEM((rows, width), BF16)],
        compiler_params=pltpu.CompilerParams(vmem_limit_bytes=VMEM_LIMIT),
        cost_estimate=pl.CostEstimate(
            flops=2 * rows * hidden * (depth + width), bytes_accessed=8 << 20, transcendentals=0
        ),
        name="project",
    )(
        features,
        w_first,
        b_first.reshape(1, hidden),
        w_second,
        b_second.reshape(1, width),
        part.reshape(1, rows),
        slot.reshape(1, rows),
        lane_base,
    )


def send_blocks(field, halo_send, send):
    for side in range(send.shape[0]):
        for k in range(send.shape[1]):
            send[side, k] = field[halo_send[side, k]]


def place_kernel(slots, half, halves, arrived, halo_send, start, send, size):
    groups = arrived.shape[0] // GROUP
    chunks = slots // PACK
    ids, rows = [], []
    filled = jnp.zeros((1, LANES), F32)
    for group in range(groups):
        sources = slice(group * GROUP, (group + 1) * GROUP)
        listed = jnp.sum(arrived[sources, halves * slots :, :].astype(F32), axis=0)
        coded = listed[:8] * 64.0 + listed[8:]
        for j in range(chunks):
            code = coded[j : j + 1, :]
            ids.append(code.astype(jnp.int32) - 1)
            filled = filled + (code > 0.0).astype(F32)
            first = half * slots + j * PACK
            rows.append(arrived[sources, first : first + PACK, :].reshape(LANES, LANES))
    ids = jnp.concatenate(ids, axis=1)
    rows = jnp.concatenate(rows, axis=0)
    size[0] = jnp.sum(filled).astype(jnp.int32)
    block_count, block_rows, _ = start.shape
    several = 4
    slot = iota((several * block_rows, ids.shape[1]), 0)
    for first in range(0, block_count, several):
        select = (slot == ids - first * block_rows).astype(BF16)
        placed = jnp.dot(select, rows, preferred_element_type=F32).astype(BF16)
        start[first : first + several] = placed.reshape(several, block_rows, LANES)
    send_blocks(start, halo_send, send)


def place(slots, half, halves, blocks, arrived, halo_send):
    block_count, block_rows = blocks
    vmem = pl.BlockSpec(memory_space=pltpu.VMEM)
    smem = pl.BlockSpec(memory_space=pltpu.SMEM)
    listed = halo_send.shape[1]
    return pl.pallas_call(
        functools.partial(place_kernel, slots, half, halves),
        out_shape=[
            jax.ShapeDtypeStruct((block_count, block_rows, LANES), BF16),
            jax.ShapeDtypeStruct((2, listed, block_rows, LANES), BF16),
            jax.ShapeDtypeStruct((1,), jnp.int32),
        ],
        in_specs=[vmem, smem],
        out_specs=[vmem, vmem, smem],
        compiler_params=pltpu.CompilerParams(vmem_limit_bytes=VMEM_LIMIT),
        cost_estimate=pl.CostEstimate(
            flops=2 * (block_count * block_rows) ** 2 * LANES, bytes_accessed=3 << 20, transcendentals=0
        ),
        name="place",
    )(arrived, halo_send)


def hop_kernel(last, *refs):
    tiles, coords, halo_send, size, start, current, low, high = refs[:8]
    if last:
        out, summed = refs[-2:]
        send = None
    else:
        out, send, summed = refs[-3:]
    block_count, block_rows, width = start.shape
    listed = low.shape[0]
    for b in range(block_count):
        summed[b] = jnp.dot(tiles[b], current[b], preferred_element_type=F32)
    first = block_count + 2 * listed
    for t in range(block_count, tiles.shape[0]):
        if t < block_count + listed:
            source = low[t - block_count]
        elif t < first:
            source = high[t - block_count - listed]
        else:
            index = coords[2 * t + 1]
            source = current[jnp.minimum(index, block_count - 1)]
            below = low[jnp.clip(index - block_count, 0, listed - 1)]
            above = high[jnp.clip(index - block_count - listed, 0, listed - 1)]
            source = jnp.where(index < block_count, source, below)
            source = jnp.where(index < block_count + listed, source, above)
        target = coords[2 * t]
        summed[target] += jnp.dot(tiles[t], source, preferred_element_type=F32)
    row = iota((block_rows, width), 0)
    for b in range(block_count):
        mixed = (1.0 - ALPHA) * summed[b] + ALPHA * start[b].astype(F32)
        mixed = jnp.where(row < size[0] - b * block_rows, mixed, 0.0).astype(BF16)
        if last:
            out[b * block_rows : (b + 1) * block_rows, :] = mixed
        else:
            out[b] = mixed
    if send is not None:
        send_blocks(out, halo_send, send)


def hop(tiles, coords, halo_send, size, start, current, low, high, half=None, halves=1, held=None):
    block_count, block_rows, width = start.shape
    listed = low.shape[0]
    last = half is not None
    vmem = pl.BlockSpec(memory_space=pltpu.VMEM)
    smem = pl.BlockSpec(memory_space=pltpu.SMEM)
    operands = [tiles, coords, halo_send, size, start, current, low, high]
    in_specs = [vmem, smem, smem, smem, vmem, vmem, vmem, vmem]
    aliases = {}
    if last:
        capacity = block_count * block_rows
        out_shape = jax.ShapeDtypeStruct((capacity, width * halves), BF16)
        out_specs = pl.BlockSpec((capacity, width), lambda i: (0, half))
        if held is not None:
            aliases = {len(operands): 0}
            operands.append(held)
            in_specs.append(pl.BlockSpec(memory_space=pl.ANY))
        in_specs = [
            spec if spec is not vmem else pl.BlockSpec(x.shape, lambda i, n=x.ndim: (0,) * n)
            for spec, x in zip(in_specs, operands)
        ]
        grid = (1,)
    else:
        out_shape = [
            jax.ShapeDtypeStruct((block_count, block_rows, width), BF16),
            jax.ShapeDtypeStruct((2, listed, block_rows, width), BF16),
        ]
        out_specs = [vmem, vmem]
        grid = ()
    return pl.pallas_call(
        functools.partial(hop_kernel, last),
        out_shape=out_shape,
        grid=grid,
        in_specs=in_specs,
        out_specs=out_specs,
        scratch_shapes=[pltpu.VMEM((block_count, block_rows, width), F32)],
        input_output_aliases=aliases,
        compiler_params=pltpu.CompilerParams(vmem_limit_bytes=VMEM_LIMIT),
        cost_estimate=pl.CostEstimate(
            flops=2 * tiles.size * width, bytes_accessed=5 << 20, transcendentals=0
        ),
        name="hop",
    )(*operands)


def local(
    features,
    w_first,
    b_first,
    w_second,
    b_second,
    dest_part,
    dest_slot,
    tile_coords,
    tile_values,
    halo_send,
):
    count_dp = lax.axis_size("dp")
    count_dom = lax.axis_size("dom")
    parts = count_dp * count_dom
    row_count = features.shape[0]
    capacity = 3 * row_count
    slots = -(-capacity // parts // PACK) * PACK
    width = w_second.shape[1]
    halves = width // LANES
    block_rows = tile_values.shape[1]
    block_count = capacity // block_rows
    me = lax.axis_index("dp") * count_dom + lax.axis_index("dom")
    lane_base = (lax.rem(me, GROUP) * PACK).astype(jnp.int32).reshape(1)
    outgoing = project(
        parts, slots, features, w_first, b_first, w_second, b_second, dest_part, dest_slot, lane_base
    )
    arrived = lax.all_to_all(outgoing, ("dp", "dom"), split_axis=0, concat_axis=0, tiled=True)
    coords = tile_coords.reshape(-1)
    lists = halo_send[0]
    forward = [(i, (i + 1) % count_dom) for i in range(count_dom)]
    backward = [((i + 1) % count_dom, i) for i in range(count_dom)]

    def exchange(send):
        return lax.ppermute(send[0], "dom", forward), lax.ppermute(send[1], "dom", backward)

    starts, fields, halos = [], [], []
    size = None
    for half in range(halves):
        start, send, size = place(slots, half, halves, (block_count, block_rows), arrived, lists)
        starts.append(start)
        fields.append(start)
        halos.append(exchange(send))
    for repeat in range(HOPS - 1):
        for half in range(halves):
            fields[half], send = hop(
                tile_values, coords, lists, size, starts[half], fields[half], *halos[half]
            )
            halos[half] = exchange(send)
    held = None
    for half in range(halves):
        held = hop(
            tile_values, coords, lists, size, starts[half], fields[half], *halos[half],
            half=half, halves=halves, held=held,
        )
    return held


def solution(mesh):
    placed = (
        P(("dp", "dom"), None),
        P(),
        P(),
        P(),
        P(),
        P(("dp", "dom")),
        P(("dp", "dom")),
        P(("dp", "dom"), None),
        P(("dp", "dom"), None, None),
        P(("dp", "dom"), None, None),
    )
    return jax.shard_map(
        local, mesh=mesh, in_specs=placed, out_specs=P(("dp", "dom"), None), check_vma=False
    )
```

```python
import functools

import jax
import jax.numpy as jnp
from jax import lax
from jax.experimental import pallas as pl
from jax.experimental.pallas import tpu as pltpu
from jax.sharding import PartitionSpec as P

HOPS = 2
ALPHA = 0.1
LANES = 128
PACK = 16
GROUP = LANES // PACK
VMEM_LIMIT = 48 * 1024 * 1024
PROJECT_VMEM = 62 * 1024 * 1024

BF16 = jnp.bfloat16
F32 = jnp.float32


def iota(shape, dim):
    return lax.broadcasted_iota(jnp.int32, shape, dim)


def gelu(value):
    return 0.5 * value * (1.0 + lax.erf(value * (0.5**0.5)))


def project_kernel(
    parts,
    slots,
    features_hbm,
    w_first_hbm,
    b_first,
    w_second_hbm,
    b_second,
    dest_part,
    dest_slot,
    lane_base,
    out,
    features,
    w_first,
    w_second,
    embedded,
    packed,
    arrival,
    leaving,
):
    copies = [
        pltpu.make_async_copy(source, held, arrival.at[index])
        for index, (source, held) in enumerate(
            ((features_hbm, features), (w_first_hbm, w_first), (w_second_hbm, w_second))
        )
    ]
    for copy in copies:
        copy.start()
    width = w_second.shape[1]
    count = dest_part.shape[0]
    part = dest_part[...][None, :]
    onehot = (iota((parts, count), 0) == part).astype(F32)
    blocks = [onehot[:, at : at + LANES] for at in range(0, count, LANES)]
    earlier = (iota((LANES, LANES), 0) < iota((LANES, LANES), 1)).astype(BF16)
    within = jnp.dot(
        jnp.concatenate(blocks, axis=0).astype(BF16), earlier, preferred_element_type=F32
    )
    offset = jnp.zeros((parts, 1), F32)
    pieces = []
    for index, piece in enumerate(blocks):
        before = within[index * parts : (index + 1) * parts, :] + offset
        pieces.append(jnp.sum(before * piece, axis=0, keepdims=True))
        offset = offset + jnp.sum(piece, axis=1, keepdims=True)
    position = jnp.concatenate(pieces, axis=1).astype(jnp.int32)
    target = part * slots + position

    coded = dest_slot[...][None, :] + 1
    high = jnp.right_shift(coded, 6)
    low = coded - high * 64
    spot = (iota((LANES, count), 0) == position).astype(BF16)
    digits = []
    for digit in (high, low):
        marked = (onehot * digit.astype(F32)).astype(BF16)
        digits.append(
            lax.dot_general(marked, spot, (((1,), (1,)), ((), ())), preferred_element_type=F32)
        )
    base = lane_base[0]
    lane = iota((parts, LANES), 1)
    mine = (lane >= base) & (lane < base + PACK)
    row = iota((parts, PACK, LANES), 1)
    listed = jnp.zeros((parts, PACK, LANES), F32)
    for at, digit in zip((0, 8), digits):
        for j in range(slots // PACK):
            turned = pltpu.roll(digit, lax.rem(base - j * PACK + LANES, LANES), 1)
            turned = jnp.where(mine, turned, 0.0)
            listed = jnp.where(row == at + j, turned[:, None, :], listed)
    halves = width // LANES
    packed[:, halves * slots :, :] = listed.astype(BF16)

    copies[0].wait()
    copies[1].wait()
    hidden = jnp.dot(features[...], w_first[...], preferred_element_type=F32)
    hidden = gelu(hidden + b_first[...].astype(F32)[None, :]).astype(BF16)
    copies[2].wait()
    total = jnp.dot(hidden, w_second[...], preferred_element_type=F32)
    embedded[...] = (total + b_second[...].astype(F32)[None, :]).astype(BF16)

    size = GROUP * slots
    slot = iota((size, count), 0)
    sends = []
    for group in range(parts // GROUP):
        select = (slot == target - group * size).astype(BF16)
        moved = jnp.dot(select, embedded[...], preferred_element_type=F32).astype(BF16)
        dests = slice(group * GROUP, (group + 1) * GROUP)
        for half in range(halves):
            piece = moved[:, half * LANES : (half + 1) * LANES]
            packed[dests, half * slots : (half + 1) * slots, :] = piece.reshape(
                GROUP, slots, LANES
            )
        sends.append(pltpu.make_async_copy(packed.at[dests], out.at[dests], leaving.at[group]))
        sends[-1].start()
    for send in sends:
        send.wait()


def project(parts, slots, features, w_first, b_first, w_second, b_second, part, slot, lane_base):
    rows, depth = features.shape
    hidden, width = w_second.shape
    length = (width // LANES) * slots + PACK
    vmem = pl.BlockSpec(memory_space=pltpu.VMEM)
    hbm = pl.BlockSpec(memory_space=pl.ANY)
    return pl.pallas_call(
        functools.partial(project_kernel, parts, slots),
        out_shape=jax.ShapeDtypeStruct((parts, length, LANES), BF16),
        in_specs=[hbm, hbm, vmem, hbm, vmem, vmem, vmem, pl.BlockSpec(memory_space=pltpu.SMEM)],
        out_specs=hbm,
        scratch_shapes=[
            pltpu.VMEM((rows, depth), BF16),
            pltpu.VMEM((depth, hidden), BF16),
            pltpu.VMEM((hidden, width), BF16),
            pltpu.VMEM((rows, width), BF16),
            pltpu.VMEM((parts, length, LANES), BF16),
            pltpu.SemaphoreType.DMA((3,)),
            pltpu.SemaphoreType.DMA((parts // GROUP,)),
        ],
        compiler_params=pltpu.CompilerParams(vmem_limit_bytes=PROJECT_VMEM),
        cost_estimate=pl.CostEstimate(
            flops=2 * rows * hidden * (depth + width), bytes_accessed=8 << 20, transcendentals=0
        ),
        name="project",
    )(features, w_first, b_first, w_second, b_second, part, slot, lane_base)


def arrived_rows(slots, halves, arrived):
    ids, rows = [], []
    for first in range(0, arrived.shape[0], GROUP):
        sources = slice(first, first + GROUP)
        listed = jnp.sum(arrived[sources, halves * slots :, :].astype(F32), axis=0)
        coded = (listed[:8] * 64.0 + listed[8:]).astype(jnp.int32)
        for j in range(slots // PACK):
            ids.append(coded[j : j + 1, :] - 1)
            pieces = []
            for half in range(halves):
                at = half * slots + j * PACK
                pieces.append(arrived[sources, at : at + PACK, :].reshape(LANES, LANES))
            rows.append(jnp.concatenate(pieces, axis=1))
    return jnp.concatenate(ids, axis=1), jnp.concatenate(rows, axis=0)


def listed_kernel(slots, halves, arrived, halo_send, *sends):
    ids, rows = arrived_rows(slots, halves, arrived)
    _, listed, block_rows, _ = sends[0].shape
    slot = iota((block_rows, ids.shape[1]), 0)
    several = 4
    for side in range(2):
        for first in range(0, listed, several):
            select = [
                (slot == ids - halo_send[side, k] * block_rows).astype(BF16)
                for k in range(first, first + several)
            ]
            placed = jnp.dot(jnp.concatenate(select, axis=0), rows, preferred_element_type=F32)
            for half, send in enumerate(sends):
                piece = placed[:, half * LANES : (half + 1) * LANES].astype(BF16)
                send[side, first : first + several] = piece.reshape(several, block_rows, LANES)


def place_kernel(slots, halves, arrived, size, *starts):
    ids, rows = arrived_rows(slots, halves, arrived)
    size[0] = jnp.sum((ids >= 0).astype(jnp.int32))
    block_count, block_rows, _ = starts[0].shape
    several = 4
    slot = iota((several * block_rows, ids.shape[1]), 0)
    for first in range(0, block_count, several):
        select = (slot == ids - first * block_rows).astype(BF16)
        placed = jnp.dot(select, rows, preferred_element_type=F32)
        for half, start in enumerate(starts):
            piece = placed[:, half * LANES : (half + 1) * LANES].astype(BF16)
            start[first : first + several] = piece.reshape(several, block_rows, LANES)


def vmem_spec():
    return pl.BlockSpec(memory_space=pltpu.VMEM)


def smem_spec():
    return pl.BlockSpec(memory_space=pltpu.SMEM)


def listed_blocks(slots, halves, block_rows, arrived, halo_send):
    listed = halo_send.shape[1]
    depth = arrived.shape[0] * slots
    return pl.pallas_call(
        functools.partial(listed_kernel, slots, halves),
        out_shape=[jax.ShapeDtypeStruct((2, listed, block_rows, LANES), BF16)] * halves,
        in_specs=[vmem_spec(), smem_spec()],
        out_specs=[vmem_spec()] * halves,
        compiler_params=pltpu.CompilerParams(vmem_limit_bytes=VMEM_LIMIT),
        cost_estimate=pl.CostEstimate(
            flops=4 * listed * block_rows * depth * halves * LANES,
            bytes_accessed=4 << 20,
            transcendentals=0,
        ),
        name="listed",
    )(arrived, halo_send)


def place(slots, halves, block_count, block_rows, arrived):
    depth = arrived.shape[0] * slots
    return pl.pallas_call(
        functools.partial(place_kernel, slots, halves),
        out_shape=[jax.ShapeDtypeStruct((1,), jnp.int32)]
        + [jax.ShapeDtypeStruct((block_count, block_rows, LANES), BF16)] * halves,
        in_specs=[vmem_spec()],
        out_specs=[smem_spec()] + [vmem_spec()] * halves,
        compiler_params=pltpu.CompilerParams(vmem_limit_bytes=VMEM_LIMIT),
        cost_estimate=pl.CostEstimate(
            flops=2 * block_count * block_rows * depth * halves * LANES,
            bytes_accessed=4 << 20,
            transcendentals=0,
        ),
        name="place",
    )(arrived)


def inner_kernel(halo, tiles, coords, start, current, partial):
    block_count = start.shape[0]
    for b in range(block_count):
        term = jnp.dot(tiles[b], current[b], preferred_element_type=F32)
        partial[b] = (1.0 - ALPHA) * term + ALPHA * start[b].astype(F32)
    for t in range(block_count + 2 * halo, tiles.shape[0]):
        index = coords[2 * t + 1]
        source = current[jnp.minimum(index, block_count - 1)]
        source = jnp.where(index < block_count, source, jnp.zeros_like(source))
        term = jnp.dot(tiles[t], source, preferred_element_type=F32)
        partial[coords[2 * t]] += (1.0 - ALPHA) * term


def outer_kernel(last, *refs):
    tiles, coords, halo_send, size, partial, low, high = refs[:7]
    if last:
        out, summed = refs[-2:]
    else:
        out, send, summed = refs[-3:]
    block_count, block_rows, width = partial.shape
    listed = low.shape[0]
    own = block_count
    summed[...] = jnp.zeros_like(summed)
    for t in range(own, tiles.shape[0]):
        if t < own + listed:
            source = low[t - own]
        elif t < own + 2 * listed:
            source = high[t - own - listed]
        else:
            index = coords[2 * t + 1]
            below = low[jnp.clip(index - own, 0, listed - 1)]
            above = high[jnp.clip(index - own - listed, 0, listed - 1)]
            source = jnp.where(index < own + listed, below, above)
            source = jnp.where(index < own, jnp.zeros_like(source), source)
        summed[coords[2 * t]] += jnp.dot(tiles[t], source, preferred_element_type=F32)
    row = iota((block_rows, width), 0)
    for b in range(block_count):
        mixed = (1.0 - ALPHA) * summed[b] + partial[b]
        mixed = jnp.where(row < size[0] - b * block_rows, mixed, 0.0).astype(BF16)
        if last:
            out[b * block_rows : (b + 1) * block_rows, :] = mixed
        else:
            out[b] = mixed
    if not last:
        for side in range(2):
            for k in range(listed):
                send[side, k] = out[halo_send[side, k]]


def inner(halo, tiles, coords, start, current):
    return pl.pallas_call(
        functools.partial(inner_kernel, halo),
        out_shape=jax.ShapeDtypeStruct(start.shape, F32),
        in_specs=[vmem_spec(), smem_spec(), vmem_spec(), vmem_spec()],
        out_specs=vmem_spec(),
        compiler_params=pltpu.CompilerParams(vmem_limit_bytes=VMEM_LIMIT),
        cost_estimate=pl.CostEstimate(
            flops=tiles.size * LANES, bytes_accessed=4 << 20, transcendentals=0
        ),
        name="inner",
    )(tiles, coords, start, current)


def outer(tiles, coords, halo_send, size, partial, low, high, half=None, halves=1, held=None):
    block_count, block_rows, width = partial.shape
    listed = low.shape[0]
    last = half is not None
    operands = [tiles, coords, halo_send, size, partial, low, high]
    vmem = vmem_spec()
    in_specs = [vmem, smem_spec(), smem_spec(), smem_spec(), vmem, vmem, vmem]
    aliases = {}
    if last:
        capacity = block_count * block_rows
        out_shape = jax.ShapeDtypeStruct((capacity, width * halves), BF16)
        out_specs = pl.BlockSpec((capacity, width), lambda i: (0, half))
        if held is not None:
            aliases = {len(operands): 0}
            operands.append(held)
            in_specs.append(pl.BlockSpec(memory_space=pl.ANY))
        in_specs = [
            spec if spec is not vmem else pl.BlockSpec(x.shape, lambda i, n=x.ndim: (0,) * n)
            for spec, x in zip(in_specs, operands)
        ]
        grid = (1,)
    else:
        out_shape = [
            jax.ShapeDtypeStruct((block_count, block_rows, width), BF16),
            jax.ShapeDtypeStruct((2, listed, block_rows, width), BF16),
        ]
        out_specs = [vmem, vmem]
        grid = ()
    return pl.pallas_call(
        functools.partial(outer_kernel, last),
        out_shape=out_shape,
        grid=grid,
        in_specs=in_specs,
        out_specs=out_specs,
        scratch_shapes=[pltpu.VMEM((block_count, block_rows, width), F32)],
        input_output_aliases=aliases,
        compiler_params=pltpu.CompilerParams(vmem_limit_bytes=VMEM_LIMIT),
        cost_estimate=pl.CostEstimate(
            flops=tiles.size * width, bytes_accessed=4 << 20, transcendentals=0
        ),
        name="outer",
    )(*operands)


def local(
    features,
    w_first,
    b_first,
    w_second,
    b_second,
    dest_part,
    dest_slot,
    tile_coords,
    tile_values,
    halo_send,
):
    count_dp = lax.axis_size("dp")
    count_dom = lax.axis_size("dom")
    parts = count_dp * count_dom
    row_count = features.shape[0]
    capacity = 3 * row_count
    slots = -(-capacity // parts // PACK) * PACK
    width = w_second.shape[1]
    halves = width // LANES
    block_rows = tile_values.shape[1]
    block_count = capacity // block_rows
    me = lax.axis_index("dp") * count_dom + lax.axis_index("dom")
    lane_base = (lax.rem(me, GROUP) * PACK).astype(jnp.int32).reshape(1)
    outgoing = project(
        parts, slots, features, w_first, b_first, w_second, b_second, dest_part, dest_slot, lane_base
    )
    arrived = lax.all_to_all(outgoing, ("dp", "dom"), split_axis=0, concat_axis=0, tiled=True)
    coords = tile_coords.reshape(-1)
    lists = halo_send[0]
    forward = [(i, (i + 1) % count_dom) for i in range(count_dom)]
    backward = [((i + 1) % count_dom, i) for i in range(count_dom)]

    def exchange(send):
        return lax.ppermute(send[0], "dom", forward), lax.ppermute(send[1], "dom", backward)

    halos = [
        exchange(send) for send in listed_blocks(slots, halves, block_rows, arrived, lists)
    ]
    size, *starts = place(slots, halves, block_count, block_rows, arrived)
    fields = list(starts)
    held = None
    for repeat in range(HOPS):
        for half in range(halves):
            partial = inner(lists.shape[1], tile_values, coords, starts[half], fields[half])
            operands = tile_values, coords, lists, size, partial, *halos[half]
            if repeat < HOPS - 1:
                fields[half], send = outer(*operands)
                halos[half] = exchange(send)
            else:
                held = outer(*operands, half=half, halves=halves, held=held)
    return held


def solution(mesh):
    placed = (
        P(("dp", "dom"), None),
        P(),
        P(),
        P(),
        P(),
        P(("dp", "dom")),
        P(("dp", "dom")),
        P(("dp", "dom"), None),
        P(("dp", "dom"), None, None),
        P(("dp", "dom"), None, None),
    )
    return jax.shard_map(
        local, mesh=mesh, in_specs=placed, out_specs=P(("dp", "dom"), None), check_vma=False
    )
```

```python
import functools

import jax
import jax.numpy as jnp
from jax import lax
from jax.experimental import pallas as pl
from jax.experimental.pallas import tpu as pltpu
from jax.sharding import PartitionSpec as P

HOPS = 2
ALPHA = 0.1
LANES = 128
PACK = 16
GROUP = LANES // PACK
FLAG = 7
VMEM_LIMIT = 48 * 1024 * 1024
PROJECT_VMEM = 62 * 1024 * 1024

BF16 = jnp.bfloat16
F32 = jnp.float32


def iota(shape, dim):
    return lax.broadcasted_iota(jnp.int32, shape, dim)


def gelu(value):
    return 0.5 * value * (1.0 + lax.erf(value * (0.5**0.5)))


def project_kernel(
    parts,
    mate,
    sizes,
    features_hbm,
    w_first_hbm,
    b_first,
    w_second_hbm,
    b_second,
    dest_part,
    dest_slot,
    lane_base,
    out,
    embedded_out,
    features,
    w_first,
    w_second,
    embedded,
    packed,
    arrival,
    leaving,
):
    direct, shared = sizes
    room = direct + shared
    slots = room + shared
    copies = [
        pltpu.make_async_copy(source, held, arrival.at[index])
        for index, (source, held) in enumerate(
            ((features_hbm, features), (w_first_hbm, w_first), (w_second_hbm, w_second))
        )
    ]
    for copy in copies:
        copy.start()
    width = w_second.shape[1]
    count = dest_part.shape[0]
    part = dest_part[...][None, :]
    onehot = (iota((parts, count), 0) == part).astype(F32)
    blocks = [onehot[:, at : at + LANES] for at in range(0, count, LANES)]
    earlier = (iota((LANES, LANES), 0) < iota((LANES, LANES), 1)).astype(BF16)
    within = jnp.dot(
        jnp.concatenate(blocks, axis=0).astype(BF16), earlier, preferred_element_type=F32
    )
    offset = jnp.zeros((parts, 1), F32)
    pieces = []
    for index, piece in enumerate(blocks):
        before = within[index * parts : (index + 1) * parts, :] + offset
        pieces.append(jnp.sum(before * piece, axis=0, keepdims=True))
        offset = offset + jnp.sum(piece, axis=1, keepdims=True)
    position = jnp.concatenate(pieces, axis=1).astype(jnp.int32)
    counts = offset
    swapped = []
    for at in range(0, parts, 2 * mate):
        swapped += [counts[at + mate : at + 2 * mate], counts[at : at + mate]]
    free = (jnp.concatenate(swapped, axis=0) <= direct).astype(F32)
    crowded = jnp.max(jnp.where(counts > room, 1.0 - free, 0.0), axis=0, keepdims=True)
    mate_free = jnp.sum(onehot * free, axis=0, keepdims=True) > 0.5
    over = position - room
    other = jnp.bitwise_xor(part, mate) * room + direct + over
    target = jnp.where(over < 0, part * room + position, jnp.where(mate_free, other, -1))

    coded = dest_slot[...][None, :] + 1
    high = jnp.right_shift(coded, 6)
    low = coded - high * 64
    spot = (iota((LANES, count), 0) == position).astype(BF16)
    digits = []
    for digit in (high, low):
        marked = (onehot * digit.astype(F32)).astype(BF16)
        digits.append(
            lax.dot_general(marked, spot, (((1,), (1,)), ((), ())), preferred_element_type=F32)
        )
    base = lane_base[0]
    lane = iota((parts, LANES), 1)
    mine = (lane >= base) & (lane < base + PACK)
    row = iota((parts, PACK, LANES), 1)
    listed = jnp.zeros((parts, PACK, LANES), F32)
    for at, digit in zip((0, 8), digits):
        for j in range(slots // PACK):
            turned = pltpu.roll(digit, lax.rem(base - j * PACK + LANES, LANES), 1)
            turned = jnp.where(mine, turned, 0.0)
            listed = jnp.where(row == at + j, turned[:, None, :], listed)
    listed = jnp.where(row == FLAG, crowded[None], listed)
    halves = width // LANES
    packed[:, halves * room :, :] = listed.astype(BF16)

    copies[0].wait()
    copies[1].wait()
    hidden = jnp.dot(features[...], w_first[...], preferred_element_type=F32)
    hidden = gelu(hidden + b_first[...].astype(F32)[None, :]).astype(BF16)
    copies[2].wait()
    total = jnp.dot(hidden, w_second[...], preferred_element_type=F32)
    embedded[...] = (total + b_second[...].astype(F32)[None, :]).astype(BF16)

    keep = pltpu.make_async_copy(embedded, embedded_out, leaving.at[parts // GROUP])
    keep.start()
    size = GROUP * room
    slot = iota((size, count), 0)
    sends = [keep]
    for group in range(parts // GROUP):
        select = (slot == target - group * size).astype(BF16)
        moved = jnp.dot(select, embedded[...], preferred_element_type=F32)
        dests = slice(group * GROUP, (group + 1) * GROUP)
        rest = []
        for half in range(halves):
            piece = moved[:, half * LANES : (half + 1) * LANES].reshape(GROUP, room, LANES)
            packed[dests, half * direct : (half + 1) * direct, :] = piece[:, :direct].astype(BF16)
            rest.append(piece[:, direct:])
        packed[dests, halves * direct : halves * room, :] = jnp.concatenate(rest, axis=1).astype(
            BF16
        )
        sends.append(pltpu.make_async_copy(packed.at[dests], out.at[dests], leaving.at[group]))
        sends[-1].start()
    for send in sends:
        send.wait()


def project(
    parts, mate, sizes, features, w_first, b_first, w_second, b_second, part, slot, lane_base
):
    rows, depth = features.shape
    hidden, width = w_second.shape
    length = (width // LANES) * sum(sizes) + PACK
    vmem = pl.BlockSpec(memory_space=pltpu.VMEM)
    hbm = pl.BlockSpec(memory_space=pl.ANY)
    return pl.pallas_call(
        functools.partial(project_kernel, parts, mate, sizes),
        out_shape=[
            jax.ShapeDtypeStruct((parts, length, LANES), BF16),
            jax.ShapeDtypeStruct((rows, width), BF16),
        ],
        in_specs=[hbm, hbm, vmem, hbm, vmem, vmem, vmem, pl.BlockSpec(memory_space=pltpu.SMEM)],
        out_specs=[hbm, hbm],
        scratch_shapes=[
            pltpu.VMEM((rows, depth), BF16),
            pltpu.VMEM((depth, hidden), BF16),
            pltpu.VMEM((hidden, width), BF16),
            pltpu.VMEM((rows, width), BF16),
            pltpu.VMEM((parts, length, LANES), BF16),
            pltpu.SemaphoreType.DMA((3,)),
            pltpu.SemaphoreType.DMA((parts // GROUP + 1,)),
        ],
        compiler_params=pltpu.CompilerParams(vmem_limit_bytes=PROJECT_VMEM),
        cost_estimate=pl.CostEstimate(
            flops=2 * rows * hidden * (depth + width), bytes_accessed=8 << 20, transcendentals=0
        ),
        name="project",
    )(features, w_first, b_first, w_second, b_second, part, slot, lane_base)


def arrived_rows(sizes, halves, arrived, extra):
    direct, shared = sizes
    room = direct + shared
    ids, rows = [], []
    for first in range(0, arrived.shape[0], GROUP):
        sources = slice(first, first + GROUP)
        listed = jnp.sum(arrived[sources, halves * room :, :].astype(F32), axis=0)
        coded = (listed[:8] * 64.0 + listed[8:]).astype(jnp.int32)
        own = arrived[sources, halves * direct : halves * room, :].astype(F32)
        more = extra[sources].astype(F32)
        rest = []
        for half in range(halves):
            part = slice(half * shared, (half + 1) * shared)
            rest.append(jnp.concatenate([own[:, part], more[:, part]], axis=1).astype(BF16))
        for j in range((room + shared) // PACK):
            ids.append(coded[j : j + 1, :] - 1)
            pieces = []
            for half in range(halves):
                at = j * PACK
                if at < direct:
                    piece = arrived[sources, half * direct + at : half * direct + at + PACK, :]
                else:
                    piece = rest[half][:, at - direct : at - direct + PACK, :]
                pieces.append(piece.reshape(LANES, LANES))
            rows.append(jnp.concatenate(pieces, axis=1))
    return jnp.concatenate(ids, axis=1), jnp.concatenate(rows, axis=0)


def listed_kernel(sizes, halves, arrived, extra, halo_send, *sends):
    ids, rows = arrived_rows(sizes, halves, arrived, extra)
    _, listed, block_rows, _ = sends[0].shape
    slot = iota((block_rows, ids.shape[1]), 0)
    several = 4
    for side in range(2):
        for first in range(0, listed, several):
            select = [
                (slot == ids - halo_send[side, k] * block_rows).astype(BF16)
                for k in range(first, first + several)
            ]
            placed = jnp.dot(jnp.concatenate(select, axis=0), rows, preferred_element_type=F32)
            for half, send in enumerate(sends):
                piece = placed[:, half * LANES : (half + 1) * LANES].astype(BF16)
                send[side, first : first + several] = piece.reshape(several, block_rows, LANES)


def place_kernel(sizes, halves, arrived, extra, size, *starts):
    ids, rows = arrived_rows(sizes, halves, arrived, extra)
    size[0] = jnp.sum((ids >= 0).astype(jnp.int32))
    block_count, block_rows, _ = starts[0].shape
    several = 4
    slot = iota((several * block_rows, ids.shape[1]), 0)
    for first in range(0, block_count, several):
        select = (slot == ids - first * block_rows).astype(BF16)
        placed = jnp.dot(select, rows, preferred_element_type=F32)
        for half, start in enumerate(starts):
            piece = placed[:, half * LANES : (half + 1) * LANES].astype(BF16)
            start[first : first + several] = piece.reshape(several, block_rows, LANES)


def vmem_spec():
    return pl.BlockSpec(memory_space=pltpu.VMEM)


def smem_spec():
    return pl.BlockSpec(memory_space=pltpu.SMEM)


def listed_blocks(sizes, halves, block_rows, arrived, extra, halo_send):
    listed = halo_send.shape[1]
    depth = arrived.shape[0] * (sizes[0] + 2 * sizes[1])
    return pl.pallas_call(
        functools.partial(listed_kernel, sizes, halves),
        out_shape=[jax.ShapeDtypeStruct((2, listed, block_rows, LANES), BF16)] * halves,
        in_specs=[vmem_spec(), vmem_spec(), smem_spec()],
        out_specs=[vmem_spec()] * halves,
        compiler_params=pltpu.CompilerParams(vmem_limit_bytes=VMEM_LIMIT),
        cost_estimate=pl.CostEstimate(
            flops=4 * listed * block_rows * depth * halves * LANES,
            bytes_accessed=4 << 20,
            transcendentals=0,
        ),
        name="listed",
    )(arrived, extra, halo_send)


def place(sizes, halves, block_count, block_rows, arrived, extra):
    depth = arrived.shape[0] * (sizes[0] + 2 * sizes[1])
    return pl.pallas_call(
        functools.partial(place_kernel, sizes, halves),
        out_shape=[jax.ShapeDtypeStruct((1,), jnp.int32)]
        + [jax.ShapeDtypeStruct((block_count, block_rows, LANES), BF16)] * halves,
        in_specs=[vmem_spec()] * 2,
        out_specs=[smem_spec()] + [vmem_spec()] * halves,
        compiler_params=pltpu.CompilerParams(vmem_limit_bytes=VMEM_LIMIT),
        cost_estimate=pl.CostEstimate(
            flops=2 * block_count * block_rows * depth * halves * LANES,
            bytes_accessed=4 << 20,
            transcendentals=0,
        ),
        name="place",
    )(arrived, extra)


def inner_kernel(halo, tiles, coords, start, current, partial):
    block_count = start.shape[0]
    for b in range(block_count):
        term = jnp.dot(tiles[b], current[b], preferred_element_type=F32)
        partial[b] = (1.0 - ALPHA) * term + ALPHA * start[b].astype(F32)
    for t in range(block_count + 2 * halo, tiles.shape[0]):
        index = coords[2 * t + 1]
        source = current[jnp.minimum(index, block_count - 1)]
        source = jnp.where(index < block_count, source, jnp.zeros_like(source))
        term = jnp.dot(tiles[t], source, preferred_element_type=F32)
        partial[coords[2 * t]] += (1.0 - ALPHA) * term


def outer_kernel(last, *refs):
    tiles, coords, halo_send, size, partial, low, high = refs[:7]
    if last:
        out, summed = refs[-2:]
    else:
        out, send, summed = refs[-3:]
    block_count, block_rows, width = partial.shape
    listed = low.shape[0]
    own = block_count
    summed[...] = jnp.zeros_like(summed)
    for t in range(own, tiles.shape[0]):
        if t < own + listed:
            source = low[t - own]
        elif t < own + 2 * listed:
            source = high[t - own - listed]
        else:
            index = coords[2 * t + 1]
            below = low[jnp.clip(index - own, 0, listed - 1)]
            above = high[jnp.clip(index - own - listed, 0, listed - 1)]
            source = jnp.where(index < own + listed, below, above)
            source = jnp.where(index < own, jnp.zeros_like(source), source)
        summed[coords[2 * t]] += jnp.dot(tiles[t], source, preferred_element_type=F32)
    row = iota((block_rows, width), 0)
    for b in range(block_count):
        mixed = (1.0 - ALPHA) * summed[b] + partial[b]
        mixed = jnp.where(row < size[0] - b * block_rows, mixed, 0.0).astype(BF16)
        if last:
            out[b * block_rows : (b + 1) * block_rows, :] = mixed
        else:
            out[b] = mixed
    if not last:
        for side in range(2):
            for k in range(listed):
                send[side, k] = out[halo_send[side, k]]


def inner(halo, tiles, coords, start, current):
    return pl.pallas_call(
        functools.partial(inner_kernel, halo),
        out_shape=jax.ShapeDtypeStruct(start.shape, F32),
        in_specs=[vmem_spec(), smem_spec(), vmem_spec(), vmem_spec()],
        out_specs=vmem_spec(),
        compiler_params=pltpu.CompilerParams(vmem_limit_bytes=VMEM_LIMIT),
        cost_estimate=pl.CostEstimate(
            flops=tiles.size * LANES, bytes_accessed=4 << 20, transcendentals=0
        ),
        name="inner",
    )(tiles, coords, start, current)


def outer(tiles, coords, halo_send, size, partial, low, high, half=None, halves=1, held=None):
    block_count, block_rows, width = partial.shape
    listed = low.shape[0]
    last = half is not None
    operands = [tiles, coords, halo_send, size, partial, low, high]
    vmem = vmem_spec()
    in_specs = [vmem, smem_spec(), smem_spec(), smem_spec(), vmem, vmem, vmem]
    aliases = {}
    if last:
        capacity = block_count * block_rows
        out_shape = jax.ShapeDtypeStruct((capacity, width * halves), BF16)
        out_specs = pl.BlockSpec((capacity, width), lambda i: (0, half))
        if held is not None:
            aliases = {len(operands): 0}
            operands.append(held)
            in_specs.append(pl.BlockSpec(memory_space=pl.ANY))
        in_specs = [
            spec if spec is not vmem else pl.BlockSpec(x.shape, lambda i, n=x.ndim: (0,) * n)
            for spec, x in zip(in_specs, operands)
        ]
        grid = (1,)
    else:
        out_shape = [
            jax.ShapeDtypeStruct((block_count, block_rows, width), BF16),
            jax.ShapeDtypeStruct((2, listed, block_rows, width), BF16),
        ]
        out_specs = [vmem, vmem]
        grid = ()
    return pl.pallas_call(
        functools.partial(outer_kernel, last),
        out_shape=out_shape,
        grid=grid,
        in_specs=in_specs,
        out_specs=out_specs,
        scratch_shapes=[pltpu.VMEM((block_count, block_rows, width), F32)],
        input_output_aliases=aliases,
        compiler_params=pltpu.CompilerParams(vmem_limit_bytes=VMEM_LIMIT),
        cost_estimate=pl.CostEstimate(
            flops=tiles.size * width, bytes_accessed=4 << 20, transcendentals=0
        ),
        name="outer",
    )(*operands)


def all_to_all(payload):
    return lax.all_to_all(payload, ("dp", "dom"), split_axis=0, concat_axis=0, tiled=True)


def late_rows(parts, sizes, embedded, dest_part):
    direct, shared = sizes
    count, width = embedded.shape
    onehot = (dest_part[:, None] == jnp.arange(parts, dtype=jnp.int32)[None, :]).astype(BF16)
    row = jnp.arange(count, dtype=jnp.int32)
    earlier = (row[None, :] < row[:, None]).astype(BF16)
    before = jnp.dot(earlier, onehot, preferred_element_type=F32)
    position = jnp.sum(before * onehot.astype(F32), axis=1).astype(jnp.int32)
    over = position - (direct + shared)
    target = jnp.where(over < 0, -1, dest_part * shared + over)
    select = (jnp.arange(parts * shared, dtype=jnp.int32)[:, None] == target[None, :]).astype(BF16)
    moved = jnp.dot(select, embedded, preferred_element_type=F32).astype(BF16)
    moved = moved.reshape(parts, shared, width // LANES, LANES)
    return jnp.swapaxes(moved, 1, 2).reshape(parts, width // LANES * shared, LANES)


def local(
    features,
    w_first,
    b_first,
    w_second,
    b_second,
    dest_part,
    dest_slot,
    tile_coords,
    tile_values,
    halo_send,
):
    count_dp = lax.axis_size("dp")
    count_dom = lax.axis_size("dom")
    parts = count_dp * count_dom
    row_count = features.shape[0]
    capacity = 3 * row_count
    most = -(-capacity // parts)
    direct = -(-most // (2 * PACK)) * PACK
    shared = max(-(-(most - direct) // 16) * 8, 8)
    sizes = direct, shared
    width = w_second.shape[1]
    halves = width // LANES
    block_rows = tile_values.shape[1]
    block_count = capacity // block_rows
    me = lax.axis_index("dp") * count_dom + lax.axis_index("dom")
    lane_base = (lax.rem(me, GROUP) * PACK).astype(jnp.int32).reshape(1)
    outgoing, embedded = project(
        parts,
        count_dom,
        sizes,
        features,
        w_first,
        b_first,
        w_second,
        b_second,
        dest_part,
        dest_slot,
        lane_base,
    )
    arrived = all_to_all(outgoing)
    crowded = jnp.any(arrived[:, halves * sum(sizes) + FLAG, :] > 0.5)
    from_mate = lax.ppermute(
        arrived[:, halves * direct : halves * sum(sizes), :],
        "dp",
        [(i, i ^ 1) for i in range(count_dp)],
    )
    extra = lax.cond(
        crowded,
        lambda: all_to_all(late_rows(parts, sizes, embedded, dest_part)),
        lambda: from_mate,
    )
    coords = tile_coords.reshape(-1)
    lists = halo_send[0]
    forward = [(i, (i + 1) % count_dom) for i in range(count_dom)]
    backward = [((i + 1) % count_dom, i) for i in range(count_dom)]

    def exchange(send):
        return lax.ppermute(send[0], "dom", forward), lax.ppermute(send[1], "dom", backward)

    halos = [
        exchange(send) for send in listed_blocks(sizes, halves, block_rows, arrived, extra, lists)
    ]
    size, *starts = place(sizes, halves, block_count, block_rows, arrived, extra)
    fields = list(starts)
    held = None
    for repeat in range(HOPS):
        for half in range(halves):
            partial = inner(lists.shape[1], tile_values, coords, starts[half], fields[half])
            operands = tile_values, coords, lists, size, partial, *halos[half]
            if repeat < HOPS - 1:
                fields[half], send = outer(*operands)
                halos[half] = exchange(send)
            else:
                held = outer(*operands, half=half, halves=halves, held=held)
    return held


def solution(mesh):
    placed = (
        P(("dp", "dom"), None),
        P(),
        P(),
        P(),
        P(),
        P(("dp", "dom")),
        P(("dp", "dom")),
        P(("dp", "dom"), None),
        P(("dp", "dom"), None, None),
        P(("dp", "dom"), None, None),
    )
    return jax.shard_map(
        local, mesh=mesh, in_specs=placed, out_specs=P(("dp", "dom"), None), check_vma=False
    )
```

```python
import functools

import jax
import jax.numpy as jnp
from jax import lax
from jax.experimental import pallas as pl
from jax.experimental.pallas import tpu as pltpu
from jax.sharding import PartitionSpec as P

HOPS = 2
ALPHA = 0.1
LANES = 128
PIECE = 8
GROUP = LANES // PIECE
DESTS = 8
FLAG = LANES - 1
POWERS = 16, 8, 4, 2, 1
OUT_BLOCKS = 6
VMEM_LIMIT = 48 * 1024 * 1024
PROJECT_VMEM = 62 * 1024 * 1024

BF16 = jnp.bfloat16
F32 = jnp.float32


def iota(shape, dim):
    return lax.broadcasted_iota(jnp.int32, shape, dim)


def gelu(value):
    return 0.5 * value * (1.0 + lax.erf(value * (0.5**0.5)))


def project_kernel(parts, mate, sizes, *refs):
    given, (out, embedded_out) = refs[:7], refs[7:9]
    held = refs[9:16]
    features, w_first, dest_part, dest_slot, b_first, w_second, b_second = held
    embedded, packed, arrival, leaving = refs[16:]
    room, direct, aligned = sizes
    own = room - 1
    copies = [
        pltpu.make_async_copy(source, kept, arrival.at[index])
        for index, (source, kept) in enumerate(zip(given, held))
    ]
    for index in (2, 3, 0, 1, 4, 5, 6):
        copies[index].start()
    copies[2].wait()
    copies[3].wait()
    width = w_second.shape[1]
    count = dest_part.shape[0]
    part = dest_part[...][None, :]
    onehot = (iota((parts, count), 0) == part).astype(F32)
    blocks = [onehot[:, at : at + LANES] for at in range(0, count, LANES)]
    earlier = (iota((LANES, LANES), 0) < iota((LANES, LANES), 1)).astype(BF16)
    within = jnp.dot(
        jnp.concatenate(blocks, axis=0).astype(BF16), earlier, preferred_element_type=F32
    )
    offset = jnp.zeros((parts, 1), F32)
    pieces = []
    for index, piece in enumerate(blocks):
        before = within[index * parts : (index + 1) * parts, :] + offset
        pieces.append(jnp.sum(before * piece, axis=0, keepdims=True))
        offset = offset + jnp.sum(piece, axis=1, keepdims=True)
    position = jnp.concatenate(pieces, axis=1).astype(jnp.int32)
    counts = offset
    swapped = []
    for at in range(0, parts, 2 * mate):
        swapped += [counts[at + mate : at + 2 * mate], counts[at : at + mate]]
    free = (jnp.concatenate(swapped, axis=0) <= direct).astype(F32)
    crowded = jnp.max(jnp.where(counts > own, 1.0 - free, 0.0), axis=0, keepdims=True)
    mate_free = jnp.sum(onehot * free, axis=0, keepdims=True) > 0.5
    over = position - own
    other = jnp.bitwise_xor(part, mate) * room + direct + over
    target = jnp.where(over < 0, part * room + position, jnp.where(mate_free, other, -1))

    slot = dest_slot[...][None, :]
    power = jnp.right_shift(slot, 7)
    code = (slot - power * 128 + 128).astype(F32)
    for bit in POWERS:
        code = jnp.where(jnp.bitwise_and(power, bit) > 0, code * 2.0**bit, code)
    place_of = jnp.where(over < 0, position, room + direct - aligned + over)
    spot = (iota((LANES, count), 0) == place_of).astype(BF16)
    coded = lax.dot_general(
        (onehot * code).astype(BF16), spot, (((1,), (1,)), ((), ())), preferred_element_type=F32
    )
    coded = jnp.where(iota((parts, LANES), 1) == FLAG, crowded, coded)

    copies[0].wait()
    copies[1].wait()
    copies[4].wait()
    hidden = jnp.dot(features[...], w_first[...], preferred_element_type=F32)
    hidden = gelu(hidden + b_first[...].astype(F32)[None, :]).astype(BF16)
    copies[5].wait()
    copies[6].wait()
    total = jnp.dot(hidden, w_second[...], preferred_element_type=F32)
    embedded[...] = (total + b_second[...].astype(F32)[None, :]).astype(BF16)

    keep = pltpu.make_async_copy(embedded, embedded_out, leaving.at[parts // DESTS])
    keep.start()
    size = DESTS * room
    halves = width // LANES
    slot = iota((size, count), 0)
    last = iota((DESTS, room, LANES), 1) == own
    sends = [keep]
    for group in range(parts // DESTS):
        select = (slot == target - group * size).astype(BF16)
        moved = jnp.dot(select, embedded[...], preferred_element_type=F32)
        dests = slice(group * DESTS, (group + 1) * DESTS)
        head, tail = [], []
        for half in range(halves):
            piece = moved[:, half * LANES : (half + 1) * LANES].reshape(DESTS, room, LANES)
            if half == 0:
                piece = jnp.where(last, coded[dests][:, None, :], piece)
            head.append(piece[:, :aligned])
            tail.append(piece[:, aligned:])
        packed[dests] = jnp.concatenate(head + tail, axis=1).astype(BF16)
        sends.append(pltpu.make_async_copy(packed.at[dests], out.at[dests], leaving.at[group]))
        sends[-1].start()
    for send in sends:
        send.wait()


def project(
    parts, mate, sizes, features, w_first, b_first, w_second, b_second, part, slot
):
    rows, depth = features.shape
    hidden, width = w_second.shape
    length = (width // LANES) * sizes[0]
    given = features, w_first, part, slot, b_first, w_second, b_second
    hbm = pl.BlockSpec(memory_space=pl.ANY)
    return pl.pallas_call(
        functools.partial(project_kernel, parts, mate, sizes),
        out_shape=[
            jax.ShapeDtypeStruct((parts, length, LANES), BF16),
            jax.ShapeDtypeStruct((rows, width), BF16),
        ],
        in_specs=[hbm] * len(given),
        out_specs=[hbm, hbm],
        scratch_shapes=[pltpu.VMEM(array.shape, array.dtype) for array in given]
        + [
            pltpu.VMEM((rows, width), BF16),
            pltpu.VMEM((parts, length, LANES), BF16),
            pltpu.SemaphoreType.DMA((len(given),)),
            pltpu.SemaphoreType.DMA((parts // DESTS + 1,)),
        ],
        compiler_params=pltpu.CompilerParams(vmem_limit_bytes=PROJECT_VMEM),
        cost_estimate=pl.CostEstimate(
            flops=2 * rows * hidden * (depth + width), bytes_accessed=8 << 20, transcendentals=0
        ),
        name="project",
    )(*given)


def arrived_rows(sizes, halves, arrived, extra):
    room, _, aligned = sizes
    beyond = room - aligned
    main = -(-2 * room // (3 * PIECE)) * PIECE
    parts = arrived.shape[0]
    found = ([], []), ([], [])
    lane = iota((GROUP, LANES), 1) // PIECE
    source = iota((GROUP, LANES), 0)
    for first in range(0, parts, GROUP):
        sources = slice(first, first + GROUP)
        got = arrived[sources].astype(F32)
        more = extra[sources].astype(F32)
        fields = []
        for half in range(halves):
            at = halves * aligned + half * beyond
            fields.append(
                jnp.concatenate(
                    [
                        got[:, half * aligned : (half + 1) * aligned],
                        got[:, at : at + beyond],
                        more[:, half * beyond : (half + 1) * beyond],
                    ],
                    axis=1,
                )
            )
        code = fields[0][:, room - 1, :]
        power = jnp.zeros_like(code)
        for bit in POWERS:
            big = code >= 128.0 * 2.0**bit
            code = jnp.where(big, code * 2.0**-bit, code)
            power = jnp.where(big, power + bit, power)
        code = jnp.where(code >= 128.0, code + 128.0 * power - 128.0, -1.0)
        turned = pltpu.roll(code, 0, 1, stride=PIECE, stride_axis=0)
        for j in range((room + beyond) // PIECE):
            row = jnp.where(lane == lax.rem(source + j, GROUP), turned, 0.0)
            row = jnp.sum(row, axis=0, keepdims=True)
            row = pltpu.roll(row, (LANES - j * PIECE) % LANES, 1)
            rows = [
                field[:, j * PIECE : (j + 1) * PIECE, :].reshape(LANES, LANES) for field in fields
            ]
            ids, kept = found[0 if (j + 1) * PIECE <= main else 1]
            ids.append(row.astype(jnp.int32))
            kept.append(jnp.concatenate(rows, axis=1).astype(BF16))
    return [(jnp.concatenate(ids, axis=1), jnp.concatenate(rows, axis=0)) for ids, rows in found]


def fill(found, refs, blocks_of):
    for turn, (ids, rows) in enumerate(found):

        def write(turn=turn, ids=ids, rows=rows):
            for places, bases in blocks_of(refs[0]):
                block_rows = refs[0].shape[-2]
                slot = iota((block_rows, ids.shape[1]), 0)
                select = [(slot == ids - base * block_rows).astype(BF16) for base in bases]
                placed = jnp.dot(
                    jnp.concatenate(select, axis=0), rows, preferred_element_type=F32
                ).astype(BF16)
                for half, ref in enumerate(refs):
                    piece = placed[:, half * LANES : (half + 1) * LANES]
                    piece = piece.reshape(len(bases), block_rows, LANES)
                    ref[places] = piece if turn == 0 else ref[places] + piece

        if turn == 0:
            write()
        else:
            pl.when(jnp.max(ids) >= 0)(write)


def listed_kernel(sizes, halves, arrived, extra, halo_send, *sends):
    def blocks_of(send):
        for side in range(2):
            for first in range(0, send.shape[1], 4):
                bases = [halo_send[side, k] for k in range(first, first + 4)]
                yield (side, slice(first, first + 4)), bases

    fill(arrived_rows(sizes, halves, arrived, extra), sends, blocks_of)


def place_kernel(sizes, halves, arrived, extra, size, *starts):
    found = arrived_rows(sizes, halves, arrived, extra)
    size[0] = sum(jnp.sum((ids >= 0).astype(jnp.int32)) for ids, _ in found)

    def blocks_of(start):
        for first in range(0, start.shape[0], 4):
            yield slice(first, first + 4), range(first, first + 4)

    fill(found, starts, blocks_of)


def vmem_spec():
    return pl.BlockSpec(memory_space=pltpu.VMEM)


def smem_spec():
    return pl.BlockSpec(memory_space=pltpu.SMEM)


def listed_blocks(sizes, halves, block_rows, arrived, extra, halo_send):
    listed = halo_send.shape[1]
    depth = arrived.shape[0] * (2 * sizes[0] - sizes[2])
    return pl.pallas_call(
        functools.partial(listed_kernel, sizes, halves),
        out_shape=[jax.ShapeDtypeStruct((2, listed, block_rows, LANES), BF16)] * halves,
        in_specs=[vmem_spec(), vmem_spec(), smem_spec()],
        out_specs=[vmem_spec()] * halves,
        compiler_params=pltpu.CompilerParams(vmem_limit_bytes=VMEM_LIMIT),
        cost_estimate=pl.CostEstimate(
            flops=4 * listed * block_rows * depth * halves * LANES,
            bytes_accessed=4 << 20,
            transcendentals=0,
        ),
        name="listed",
    )(arrived, extra, halo_send)


def place(sizes, halves, block_count, block_rows, arrived, extra):
    depth = arrived.shape[0] * (2 * sizes[0] - sizes[2])
    return pl.pallas_call(
        functools.partial(place_kernel, sizes, halves),
        out_shape=[jax.ShapeDtypeStruct((1,), jnp.int32)]
        + [jax.ShapeDtypeStruct((block_count, block_rows, LANES), BF16)] * halves,
        in_specs=[vmem_spec()] * 2,
        out_specs=[smem_spec()] + [vmem_spec()] * halves,
        compiler_params=pltpu.CompilerParams(vmem_limit_bytes=VMEM_LIMIT),
        cost_estimate=pl.CostEstimate(
            flops=2 * block_count * block_rows * depth * halves * LANES,
            bytes_accessed=4 << 20,
            transcendentals=0,
        ),
        name="place",
    )(arrived, extra)


def inner_kernel(halo, tiles, coords, start, current, partial):
    block_count = start.shape[0]
    for b in range(block_count):
        term = jnp.dot(tiles[b], current[b], preferred_element_type=F32)
        partial[b] = (1.0 - ALPHA) * term + ALPHA * start[b].astype(F32)
    for t in range(block_count + 2 * halo, tiles.shape[0]):
        index = coords[2 * t + 1]
        source = current[jnp.minimum(index, block_count - 1)]
        source = jnp.where(index < block_count, source, jnp.zeros_like(source))
        term = jnp.dot(tiles[t], source, preferred_element_type=F32)
        partial[coords[2 * t]] += (1.0 - ALPHA) * term


def outer_kernel(half, *refs):
    tiles, coords, halo_send, size, partial, low, high = refs[:7]
    if half is None:
        out, send, terms, summed = refs[-4:]
    else:
        out, terms, summed, rounded, leaving = refs[-5:]
    block_count, block_rows, width = partial.shape
    listed = low.shape[0]
    own = block_count
    for t in range(own, tiles.shape[0]):
        if t < own + listed:
            source = low[t - own]
        elif t < own + 2 * listed:
            source = high[t - own - listed]
        else:
            index = coords[2 * t + 1]
            below = low[jnp.clip(index - own, 0, listed - 1)]
            above = high[jnp.clip(index - own - listed, 0, listed - 1)]
            source = jnp.where(index < own + listed, below, above)
            source = jnp.where(index < own, jnp.zeros_like(source), source)
        terms[t - own] = jnp.dot(tiles[t], source, preferred_element_type=F32)
    summed[...] = partial[...]
    for t in range(own, tiles.shape[0]):
        summed[coords[2 * t]] += (1.0 - ALPHA) * terms[t - own]
    row = iota((block_rows, width), 0)
    copies = []
    for b in range(block_count):
        mixed = jnp.where(row < size[0] - b * block_rows, summed[b], 0.0).astype(BF16)
        if half is None:
            out[b] = mixed
            continue
        rounded[b * block_rows : (b + 1) * block_rows, :] = mixed
        if (b + 1) % OUT_BLOCKS == 0:
            rows = slice((b + 1 - OUT_BLOCKS) * block_rows, (b + 1) * block_rows)
            columns = slice(half * width, (half + 1) * width)
            copies.append(
                pltpu.make_async_copy(
                    rounded.at[rows], out.at[rows, columns], leaving.at[len(copies)]
                )
            )
            copies[-1].start()
    for copy in copies:
        copy.wait()
    if half is None:
        for side in range(2):
            for k in range(listed):
                send[side, k] = out[halo_send[side, k]]


def inner(halo, tiles, coords, start, current):
    return pl.pallas_call(
        functools.partial(inner_kernel, halo),
        out_shape=jax.ShapeDtypeStruct(start.shape, F32),
        in_specs=[vmem_spec(), smem_spec(), vmem_spec(), vmem_spec()],
        out_specs=vmem_spec(),
        compiler_params=pltpu.CompilerParams(vmem_limit_bytes=VMEM_LIMIT),
        cost_estimate=pl.CostEstimate(
            flops=tiles.size * LANES, bytes_accessed=4 << 20, transcendentals=0
        ),
        name="inner",
    )(tiles, coords, start, current)


def outer(tiles, coords, halo_send, size, partial, low, high, half=None, halves=1, held=None):
    block_count, block_rows, width = partial.shape
    listed = low.shape[0]
    operands = [tiles, coords, halo_send, size, partial, low, high]
    vmem = vmem_spec()
    in_specs = [vmem, smem_spec(), smem_spec(), smem_spec(), vmem, vmem, vmem]
    scratch = [
        pltpu.VMEM((tiles.shape[0] - block_count, block_rows, width), F32),
        pltpu.VMEM((block_count, block_rows, width), F32),
    ]
    aliases = {}
    if half is None:
        out_shape = [
            jax.ShapeDtypeStruct((block_count, block_rows, width), BF16),
            jax.ShapeDtypeStruct((2, listed, block_rows, width), BF16),
        ]
        out_specs = [vmem, vmem]
    else:
        capacity = block_count * block_rows
        out_shape = jax.ShapeDtypeStruct((capacity, width * halves), BF16)
        out_specs = pl.BlockSpec(memory_space=pl.ANY)
        scratch += [
            pltpu.VMEM((capacity, width), BF16),
            pltpu.SemaphoreType.DMA((block_count // OUT_BLOCKS,)),
        ]
        if held is not None:
            aliases = {len(operands): 0}
            operands.append(held)
            in_specs.append(pl.BlockSpec(memory_space=pl.ANY))
    return pl.pallas_call(
        functools.partial(outer_kernel, half),
        out_shape=out_shape,
        in_specs=in_specs,
        out_specs=out_specs,
        scratch_shapes=scratch,
        input_output_aliases=aliases,
        compiler_params=pltpu.CompilerParams(vmem_limit_bytes=VMEM_LIMIT),
        cost_estimate=pl.CostEstimate(
            flops=tiles.size * width, bytes_accessed=4 << 20, transcendentals=0
        ),
        name="outer",
    )(*operands)


def all_to_all(payload):
    return lax.all_to_all(payload, ("dp", "dom"), split_axis=0, concat_axis=0, tiled=True)


def late_rows(parts, sizes, embedded, dest_part):
    room, direct, aligned = sizes
    shared = room - aligned
    count, width = embedded.shape
    onehot = (dest_part[:, None] == jnp.arange(parts, dtype=jnp.int32)[None, :]).astype(BF16)
    row = jnp.arange(count, dtype=jnp.int32)
    earlier = (row[None, :] < row[:, None]).astype(BF16)
    before = jnp.dot(earlier, onehot, preferred_element_type=F32)
    position = jnp.sum(before * onehot.astype(F32), axis=1).astype(jnp.int32)
    over = position - (room - 1)
    target = jnp.where(over < 0, -1, dest_part * shared + direct - aligned + over)
    select = (jnp.arange(parts * shared, dtype=jnp.int32)[:, None] == target[None, :]).astype(BF16)
    moved = jnp.dot(select, embedded, preferred_element_type=F32).astype(BF16)
    moved = moved.reshape(parts, shared, width // LANES, LANES)
    return jnp.swapaxes(moved, 1, 2).reshape(parts, width // LANES * shared, LANES)


def local(
    features,
    w_first,
    b_first,
    w_second,
    b_second,
    dest_part,
    dest_slot,
    tile_coords,
    tile_values,
    halo_send,
):
    count_dp = lax.axis_size("dp")
    count_dom = lax.axis_size("dom")
    parts = count_dp * count_dom
    row_count = features.shape[0]
    capacity = 3 * row_count
    most = -(-capacity // parts)
    room = -(-3 * most // 32) * 8
    direct = 2 * (room - 1) - most
    sizes = room, direct, direct // 8 * 8
    width = w_second.shape[1]
    halves = width // LANES
    block_rows = tile_values.shape[1]
    block_count = capacity // block_rows
    outgoing, embedded = project(
        parts,
        count_dom,
        sizes,
        features,
        w_first,
        b_first,
        w_second,
        b_second,
        dest_part,
        dest_slot,
    )
    arrived = all_to_all(outgoing)
    codes = halves * sizes[2] + (room - sizes[2]) - 1
    crowded = jnp.any(arrived[:, codes, FLAG] > 0.5)
    from_mate = lax.ppermute(
        arrived[:, halves * sizes[2] :, :],
        "dp",
        [(i, i ^ 1) for i in range(count_dp)],
    )
    extra = lax.cond(
        crowded,
        lambda: all_to_all(late_rows(parts, sizes, embedded, dest_part)),
        lambda: from_mate,
    )
    coords = tile_coords.reshape(-1)
    lists = halo_send[0]
    forward = [(i, (i + 1) % count_dom) for i in range(count_dom)]
    backward = [((i + 1) % count_dom, i) for i in range(count_dom)]

    def exchange(send):
        return lax.ppermute(send[0], "dom", forward), lax.ppermute(send[1], "dom", backward)

    halos = [
        exchange(send) for send in listed_blocks(sizes, halves, block_rows, arrived, extra, lists)
    ]
    size, *starts = place(sizes, halves, block_count, block_rows, arrived, extra)
    fields = list(starts)
    held = None
    for repeat in range(HOPS):
        for half in range(halves):
            partial = inner(lists.shape[1], tile_values, coords, starts[half], fields[half])
            operands = tile_values, coords, lists, size, partial, *halos[half]
            if repeat < HOPS - 1:
                fields[half], send = outer(*operands)
                halos[half] = exchange(send)
            else:
                held = outer(*operands, half=half, halves=halves, held=held)
    return held


def solution(mesh):
    placed = (
        P(("dp", "dom"), None),
        P(),
        P(),
        P(),
        P(),
        P(("dp", "dom")),
        P(("dp", "dom")),
        P(("dp", "dom"), None),
        P(("dp", "dom"), None, None),
        P(("dp", "dom"), None, None),
    )
    return jax.shard_map(
        local, mesh=mesh, in_specs=placed, out_specs=P(("dp", "dom"), None), check_vma=False
    )
```

```python
import functools

import jax
import jax.numpy as jnp
from jax import lax
from jax.experimental import pallas as pl
from jax.experimental.pallas import tpu as pltpu
from jax.sharding import PartitionSpec as P

HOPS = 2
ALPHA = 0.1
LANES = 128
PIECE = 8
GROUP = LANES // PIECE
DESTS = 8
FLAG = LANES - 1
POWERS = 16, 8, 4, 2, 1
OUT_BLOCKS = 6
VMEM_LIMIT = 48 * 1024 * 1024
PROJECT_VMEM = 62 * 1024 * 1024

BF16 = jnp.bfloat16
F32 = jnp.float32


def iota(shape, dim):
    return lax.broadcasted_iota(jnp.int32, shape, dim)


def gelu(value):
    return 0.5 * value * (1.0 + lax.erf(value * (0.5**0.5)))


def project_kernel(parts, mate, sizes, *refs):
    given, (out, embedded_out) = refs[:7], refs[7:9]
    held = refs[9:16]
    features, w_first, dest_part, dest_slot, b_first, w_second, b_second = held
    embedded, packed, arrival, leaving = refs[16:]
    room, direct, aligned = sizes
    own = room - 1
    copies = [
        pltpu.make_async_copy(source, kept, arrival.at[index])
        for index, (source, kept) in enumerate(zip(given, held))
    ]
    for index in (2, 3, 0, 1, 4, 5, 6):
        copies[index].start()
    copies[2].wait()
    copies[3].wait()
    width = w_second.shape[1]
    count = dest_part.shape[0]
    part = dest_part[...][None, :]
    onehot = (iota((parts, count), 0) == part).astype(F32)
    blocks = [onehot[:, at : at + LANES] for at in range(0, count, LANES)]
    earlier = (iota((LANES, LANES), 0) < iota((LANES, LANES), 1)).astype(BF16)
    within = jnp.dot(
        jnp.concatenate(blocks, axis=0).astype(BF16), earlier, preferred_element_type=F32
    )
    offset = jnp.zeros((parts, 1), F32)
    pieces = []
    for index, piece in enumerate(blocks):
        before = within[index * parts : (index + 1) * parts, :] + offset
        pieces.append(jnp.sum(before * piece, axis=0, keepdims=True))
        offset = offset + jnp.sum(piece, axis=1, keepdims=True)
    position = jnp.concatenate(pieces, axis=1).astype(jnp.int32)
    counts = offset
    swapped = []
    for at in range(0, parts, 2 * mate):
        swapped += [counts[at + mate : at + 2 * mate], counts[at : at + mate]]
    free = (jnp.concatenate(swapped, axis=0) <= direct).astype(F32)
    crowded = jnp.max(jnp.where(counts > own, 1.0 - free, 0.0), axis=0, keepdims=True)
    mate_free = jnp.sum(onehot * free, axis=0, keepdims=True) > 0.5
    over = position - own
    other = jnp.bitwise_xor(part, mate) * room + direct + over
    target = jnp.where(over < 0, part * room + position, jnp.where(mate_free, other, -1))

    slot = dest_slot[...][None, :]
    power = jnp.right_shift(slot, 7)
    code = (slot - power * 128 + 128).astype(F32)
    for bit in POWERS:
        code = jnp.where(jnp.bitwise_and(power, bit) > 0, code * 2.0**bit, code)
    place_of = jnp.where(over < 0, position, room + direct - aligned + over)
    spot = (iota((LANES, count), 0) == place_of).astype(BF16)
    coded = lax.dot_general(
        (onehot * code).astype(BF16), spot, (((1,), (1,)), ((), ())), preferred_element_type=F32
    )
    coded = jnp.where(iota((parts, LANES), 1) == FLAG, crowded, coded)

    copies[0].wait()
    copies[1].wait()
    copies[4].wait()
    hidden = jnp.dot(features[...], w_first[...], preferred_element_type=F32)
    copies[5].wait()
    copies[6].wait()
    totals = []
    half_rows = count // 2
    for first in range(0, count, half_rows):
        piece = hidden[first : first + half_rows] + b_first[...].astype(F32)[None, :]
        piece = gelu(piece).astype(BF16)
        totals.append(jnp.dot(piece, w_second[...], preferred_element_type=F32))
    total = jnp.concatenate(totals, axis=0)
    embedded[...] = (total + b_second[...].astype(F32)[None, :]).astype(BF16)

    keep = pltpu.make_async_copy(embedded, embedded_out, leaving.at[parts // DESTS])
    keep.start()
    size = DESTS * room
    halves = width // LANES
    slot = iota((size, count), 0)
    last = iota((DESTS, room, LANES), 1) == own
    sends = [keep]
    for group in range(parts // DESTS):
        select = (slot == target - group * size).astype(BF16)
        moved = jnp.dot(select, embedded[...], preferred_element_type=F32)
        dests = slice(group * DESTS, (group + 1) * DESTS)
        head, tail = [], []
        for half in range(halves):
            piece = moved[:, half * LANES : (half + 1) * LANES].reshape(DESTS, room, LANES)
            if half == 0:
                piece = jnp.where(last, coded[dests][:, None, :], piece)
            head.append(piece[:, :aligned])
            tail.append(piece[:, aligned:])
        packed[dests] = jnp.concatenate(head + tail, axis=1).astype(BF16)
        sends.append(pltpu.make_async_copy(packed.at[dests], out.at[dests], leaving.at[group]))
        sends[-1].start()
    for send in sends:
        send.wait()


def project(
    parts, mate, sizes, features, w_first, b_first, w_second, b_second, part, slot
):
    rows, depth = features.shape
    hidden, width = w_second.shape
    length = (width // LANES) * sizes[0]
    given = features, w_first, part, slot, b_first, w_second, b_second
    hbm = pl.BlockSpec(memory_space=pl.ANY)
    return pl.pallas_call(
        functools.partial(project_kernel, parts, mate, sizes),
        out_shape=[
            jax.ShapeDtypeStruct((parts, length, LANES), BF16),
            jax.ShapeDtypeStruct((rows, width), BF16),
        ],
        in_specs=[hbm] * len(given),
        out_specs=[hbm, hbm],
        scratch_shapes=[pltpu.VMEM(array.shape, array.dtype) for array in given]
        + [
            pltpu.VMEM((rows, width), BF16),
            pltpu.VMEM((parts, length, LANES), BF16),
            pltpu.SemaphoreType.DMA((len(given),)),
            pltpu.SemaphoreType.DMA((parts // DESTS + 1,)),
        ],
        compiler_params=pltpu.CompilerParams(vmem_limit_bytes=PROJECT_VMEM),
        cost_estimate=pl.CostEstimate(
            flops=2 * rows * hidden * (depth + width), bytes_accessed=8 << 20, transcendentals=0
        ),
        name="project",
    )(*given)


def arrived_rows(sizes, halves, arrived, extra):
    room, _, aligned = sizes
    beyond = room - aligned
    main = -(-2 * room // (3 * PIECE)) * PIECE
    parts = arrived.shape[0]
    found = ([], []), ([], [])
    lane = iota((GROUP, LANES), 1) // PIECE
    source = iota((GROUP, LANES), 0)
    for first in range(0, parts, GROUP):
        sources = slice(first, first + GROUP)
        got = arrived[sources].astype(F32)
        more = extra[sources].astype(F32)
        fields = []
        for half in range(halves):
            at = halves * aligned + half * beyond
            fields.append(
                jnp.concatenate(
                    [
                        got[:, half * aligned : (half + 1) * aligned],
                        got[:, at : at + beyond],
                        more[:, half * beyond : (half + 1) * beyond],
                    ],
                    axis=1,
                )
            )
        code = fields[0][:, room - 1, :]
        power = jnp.zeros_like(code)
        for bit in POWERS:
            big = code >= 128.0 * 2.0**bit
            code = jnp.where(big, code * 2.0**-bit, code)
            power = jnp.where(big, power + bit, power)
        code = jnp.where(code >= 128.0, code + 128.0 * power - 128.0, -1.0)
        turned = pltpu.roll(code, 0, 1, stride=PIECE, stride_axis=0)
        for j in range((room + beyond) // PIECE):
            row = jnp.where(lane == lax.rem(source + j, GROUP), turned, 0.0)
            row = jnp.sum(row, axis=0, keepdims=True)
            row = pltpu.roll(row, (LANES - j * PIECE) % LANES, 1)
            rows = [
                field[:, j * PIECE : (j + 1) * PIECE, :].reshape(LANES, LANES) for field in fields
            ]
            ids, kept = found[0 if (j + 1) * PIECE <= main else 1]
            ids.append(row.astype(jnp.int32))
            kept.append(jnp.concatenate(rows, axis=1).astype(BF16))
    return [(jnp.concatenate(ids, axis=1), jnp.concatenate(rows, axis=0)) for ids, rows in found]


def fill(found, refs, blocks_of):
    for turn, (ids, rows) in enumerate(found):

        def write(turn=turn, ids=ids, rows=rows):
            for places, bases in blocks_of(refs[0]):
                block_rows = refs[0].shape[-2]
                slot = iota((block_rows, ids.shape[1]), 0)
                select = [(slot == ids - base * block_rows).astype(BF16) for base in bases]
                placed = jnp.dot(
                    jnp.concatenate(select, axis=0), rows, preferred_element_type=F32
                ).astype(BF16)
                for half, ref in enumerate(refs):
                    piece = placed[:, half * LANES : (half + 1) * LANES]
                    piece = piece.reshape(len(bases), block_rows, LANES)
                    ref[places] = piece if turn == 0 else ref[places] + piece

        if turn == 0:
            write()
        else:
            pl.when(jnp.max(ids) >= 0)(write)


def listed_kernel(sizes, halves, arrived, extra, halo_send, *sends):
    def blocks_of(send):
        for side in range(2):
            for first in range(0, send.shape[1], 4):
                bases = [halo_send[side, k] for k in range(first, first + 4)]
                yield (side, slice(first, first + 4)), bases

    fill(arrived_rows(sizes, halves, arrived, extra), sends, blocks_of)


def place_kernel(sizes, halves, arrived, extra, size, *starts):
    found = arrived_rows(sizes, halves, arrived, extra)
    size[0] = sum(jnp.sum((ids >= 0).astype(jnp.int32)) for ids, _ in found)

    def blocks_of(start):
        for first in range(0, start.shape[0], 4):
            yield slice(first, first + 4), range(first, first + 4)

    fill(found, starts, blocks_of)


def vmem_spec():
    return pl.BlockSpec(memory_space=pltpu.VMEM)


def smem_spec():
    return pl.BlockSpec(memory_space=pltpu.SMEM)


def listed_blocks(sizes, halves, block_rows, arrived, extra, halo_send):
    listed = halo_send.shape[1]
    depth = arrived.shape[0] * (2 * sizes[0] - sizes[2])
    return pl.pallas_call(
        functools.partial(listed_kernel, sizes, halves),
        out_shape=[jax.ShapeDtypeStruct((2, listed, block_rows, LANES), BF16)] * halves,
        in_specs=[vmem_spec(), vmem_spec(), smem_spec()],
        out_specs=[vmem_spec()] * halves,
        compiler_params=pltpu.CompilerParams(vmem_limit_bytes=VMEM_LIMIT),
        cost_estimate=pl.CostEstimate(
            flops=4 * listed * block_rows * depth * halves * LANES,
            bytes_accessed=4 << 20,
            transcendentals=0,
        ),
        name="listed",
    )(arrived, extra, halo_send)


def place(sizes, halves, block_count, block_rows, arrived, extra):
    depth = arrived.shape[0] * (2 * sizes[0] - sizes[2])
    return pl.pallas_call(
        functools.partial(place_kernel, sizes, halves),
        out_shape=[jax.ShapeDtypeStruct((1,), jnp.int32)]
        + [jax.ShapeDtypeStruct((block_count, block_rows, LANES), BF16)] * halves,
        in_specs=[vmem_spec()] * 2,
        out_specs=[smem_spec()] + [vmem_spec()] * halves,
        compiler_params=pltpu.CompilerParams(vmem_limit_bytes=VMEM_LIMIT),
        cost_estimate=pl.CostEstimate(
            flops=2 * block_count * block_rows * depth * halves * LANES,
            bytes_accessed=4 << 20,
            transcendentals=0,
        ),
        name="place",
    )(arrived, extra)


def inner_kernel(halo, tiles, coords, start, current, partial):
    block_count = start.shape[0]
    for b in range(block_count):
        term = jnp.dot(tiles[b], current[b], preferred_element_type=F32)
        partial[b] = (1.0 - ALPHA) * term + ALPHA * start[b].astype(F32)
    for t in range(block_count + 2 * halo, tiles.shape[0]):
        index = coords[2 * t + 1]
        source = current[jnp.minimum(index, block_count - 1)]
        source = jnp.where(index < block_count, source, jnp.zeros_like(source))
        term = jnp.dot(tiles[t], source, preferred_element_type=F32)
        partial[coords[2 * t]] += (1.0 - ALPHA) * term


def outer_kernel(half, *refs):
    tiles, coords, halo_send, size, partial, low, high = refs[:7]
    if half is None:
        out, send, terms, summed = refs[-4:]
    else:
        out, terms, summed, rounded, leaving = refs[-5:]
    block_count, block_rows, width = partial.shape
    listed = low.shape[0]
    own = block_count
    for t in range(own, tiles.shape[0]):
        if t < own + listed:
            source = low[t - own]
        elif t < own + 2 * listed:
            source = high[t - own - listed]
        else:
            index = coords[2 * t + 1]
            below = low[jnp.clip(index - own, 0, listed - 1)]
            above = high[jnp.clip(index - own - listed, 0, listed - 1)]
            source = jnp.where(index < own + listed, below, above)
            source = jnp.where(index < own, jnp.zeros_like(source), source)
        terms[t - own] = jnp.dot(tiles[t], source, preferred_element_type=F32)
    summed[...] = partial[...]
    for t in range(own, tiles.shape[0]):
        summed[coords[2 * t]] += (1.0 - ALPHA) * terms[t - own]
    row = iota((block_rows, width), 0)
    copies = []
    for b in range(block_count):
        mixed = jnp.where(row < size[0] - b * block_rows, summed[b], 0.0).astype(BF16)
        if half is None:
            out[b] = mixed
            continue
        rounded[b * block_rows : (b + 1) * block_rows, :] = mixed
        if (b + 1) % OUT_BLOCKS == 0:
            rows = slice((b + 1 - OUT_BLOCKS) * block_rows, (b + 1) * block_rows)
            columns = slice(half * width, (half + 1) * width)
            copies.append(
                pltpu.make_async_copy(
                    rounded.at[rows], out.at[rows, columns], leaving.at[len(copies)]
                )
            )
            copies[-1].start()
    for copy in copies:
        copy.wait()
    if half is None:
        for side in range(2):
            for k in range(listed):
                send[side, k] = out[halo_send[side, k]]


def inner(halo, tiles, coords, start, current):
    return pl.pallas_call(
        functools.partial(inner_kernel, halo),
        out_shape=jax.ShapeDtypeStruct(start.shape, F32),
        in_specs=[vmem_spec(), smem_spec(), vmem_spec(), vmem_spec()],
        out_specs=vmem_spec(),
        compiler_params=pltpu.CompilerParams(vmem_limit_bytes=VMEM_LIMIT),
        cost_estimate=pl.CostEstimate(
            flops=tiles.size * LANES, bytes_accessed=4 << 20, transcendentals=0
        ),
        name="inner",
    )(tiles, coords, start, current)


def outer(tiles, coords, halo_send, size, partial, low, high, half=None, halves=1, held=None):
    block_count, block_rows, width = partial.shape
    listed = low.shape[0]
    operands = [tiles, coords, halo_send, size, partial, low, high]
    vmem = vmem_spec()
    in_specs = [vmem, smem_spec(), smem_spec(), smem_spec(), vmem, vmem, vmem]
    scratch = [
        pltpu.VMEM((tiles.shape[0] - block_count, block_rows, width), F32),
        pltpu.VMEM((block_count, block_rows, width), F32),
    ]
    aliases = {}
    if half is None:
        out_shape = [
            jax.ShapeDtypeStruct((block_count, block_rows, width), BF16),
            jax.ShapeDtypeStruct((2, listed, block_rows, width), BF16),
        ]
        out_specs = [vmem, vmem]
    else:
        capacity = block_count * block_rows
        out_shape = jax.ShapeDtypeStruct((capacity, width * halves), BF16)
        out_specs = pl.BlockSpec(memory_space=pl.ANY)
        scratch += [
            pltpu.VMEM((capacity, width), BF16),
            pltpu.SemaphoreType.DMA((block_count // OUT_BLOCKS,)),
        ]
        if held is not None:
            aliases = {len(operands): 0}
            operands.append(held)
            in_specs.append(pl.BlockSpec(memory_space=pl.ANY))
    return pl.pallas_call(
        functools.partial(outer_kernel, half),
        out_shape=out_shape,
        in_specs=in_specs,
        out_specs=out_specs,
        scratch_shapes=scratch,
        input_output_aliases=aliases,
        compiler_params=pltpu.CompilerParams(vmem_limit_bytes=VMEM_LIMIT),
        cost_estimate=pl.CostEstimate(
            flops=tiles.size * width, bytes_accessed=4 << 20, transcendentals=0
        ),
        name="outer",
    )(*operands)


def all_to_all(payload):
    return lax.all_to_all(payload, ("dp", "dom"), split_axis=0, concat_axis=0, tiled=True)


def late_rows(parts, sizes, embedded, dest_part):
    room, direct, aligned = sizes
    shared = room - aligned
    count, width = embedded.shape
    onehot = (dest_part[:, None] == jnp.arange(parts, dtype=jnp.int32)[None, :]).astype(BF16)
    row = jnp.arange(count, dtype=jnp.int32)
    earlier = (row[None, :] < row[:, None]).astype(BF16)
    before = jnp.dot(earlier, onehot, preferred_element_type=F32)
    position = jnp.sum(before * onehot.astype(F32), axis=1).astype(jnp.int32)
    over = position - (room - 1)
    target = jnp.where(over < 0, -1, dest_part * shared + direct - aligned + over)
    select = (jnp.arange(parts * shared, dtype=jnp.int32)[:, None] == target[None, :]).astype(BF16)
    moved = jnp.dot(select, embedded, preferred_element_type=F32).astype(BF16)
    moved = moved.reshape(parts, shared, width // LANES, LANES)
    return jnp.swapaxes(moved, 1, 2).reshape(parts, width // LANES * shared, LANES)


def local(
    features,
    w_first,
    b_first,
    w_second,
    b_second,
    dest_part,
    dest_slot,
    tile_coords,
    tile_values,
    halo_send,
):
    count_dp = lax.axis_size("dp")
    count_dom = lax.axis_size("dom")
    parts = count_dp * count_dom
    row_count = features.shape[0]
    capacity = 3 * row_count
    most = -(-capacity // parts)
    room = -(-3 * most // 32) * 8
    direct = 2 * (room - 1) - most
    sizes = room, direct, direct // 8 * 8
    width = w_second.shape[1]
    halves = width // LANES
    block_rows = tile_values.shape[1]
    block_count = capacity // block_rows
    outgoing, embedded = project(
        parts,
        count_dom,
        sizes,
        features,
        w_first,
        b_first,
        w_second,
        b_second,
        dest_part,
        dest_slot,
    )
    arrived = all_to_all(outgoing)
    codes = halves * sizes[2] + (room - sizes[2]) - 1
    crowded = jnp.any(arrived[:, codes, FLAG] > 0.5)
    from_mate = lax.ppermute(
        arrived[:, halves * sizes[2] :, :],
        "dp",
        [(i, i ^ 1) for i in range(count_dp)],
    )
    extra = lax.cond(
        crowded,
        lambda: all_to_all(late_rows(parts, sizes, embedded, dest_part)),
        lambda: from_mate,
    )
    coords = tile_coords.reshape(-1)
    lists = halo_send[0]
    forward = [(i, (i + 1) % count_dom) for i in range(count_dom)]
    backward = [((i + 1) % count_dom, i) for i in range(count_dom)]

    def exchange(send):
        return lax.ppermute(send[0], "dom", forward), lax.ppermute(send[1], "dom", backward)

    halos = [
        exchange(send) for send in listed_blocks(sizes, halves, block_rows, arrived, extra, lists)
    ]
    size, *starts = place(sizes, halves, block_count, block_rows, arrived, extra)
    fields = list(starts)
    held = None
    for repeat in range(HOPS):
        for half in range(halves):
            partial = inner(lists.shape[1], tile_values, coords, starts[half], fields[half])
            operands = tile_values, coords, lists, size, partial, *halos[half]
            if repeat < HOPS - 1:
                fields[half], send = outer(*operands)
                halos[half] = exchange(send)
            else:
                held = outer(*operands, half=half, halves=halves, held=held)
    return held


def solution(mesh):
    placed = (
        P(("dp", "dom"), None),
        P(),
        P(),
        P(),
        P(),
        P(("dp", "dom")),
        P(("dp", "dom")),
        P(("dp", "dom"), None),
        P(("dp", "dom"), None, None),
        P(("dp", "dom"), None, None),
    )
    return jax.shard_map(
        local, mesh=mesh, in_specs=placed, out_specs=P(("dp", "dom"), None), check_vma=False
    )
```

```python
import functools

import jax
import jax.numpy as jnp
from jax import lax
from jax.experimental import pallas as pl
from jax.experimental.pallas import tpu as pltpu
from jax.sharding import PartitionSpec as P

HOPS = 2
ALPHA = 0.1
LANES = 128
PIECE = 8
GROUP = LANES // PIECE
DESTS = 8
FLAG = LANES - 1
POWERS = 16, 8, 4, 2, 1
OUT_BLOCKS = 6
VMEM_LIMIT = 48 * 1024 * 1024
PROJECT_VMEM = 62 * 1024 * 1024

BF16 = jnp.bfloat16
F32 = jnp.float32


def iota(shape, dim):
    return lax.broadcasted_iota(jnp.int32, shape, dim)


def gelu(value):
    return 0.5 * value * (1.0 + lax.erf(value * (0.5**0.5)))


def project_kernel(parts, mate, sizes, *refs):
    given, (out, embedded_out) = refs[:7], refs[7:9]
    held = refs[9:16]
    features, w_first, dest_part, dest_slot, b_first, w_second, b_second = held
    embedded, packed, arrival, leaving = refs[16:]
    room, direct, aligned = sizes
    copies = [
        pltpu.make_async_copy(source, kept, arrival.at[index])
        for index, (source, kept) in enumerate(zip(given, held))
    ]
    for index in (2, 3, 0, 1, 4, 5, 6):
        copies[index].start()
    copies[2].wait()
    copies[3].wait()
    width = w_second.shape[1]
    count = dest_part.shape[0]
    part = dest_part[...][None, :]
    onehot = (iota((parts, count), 0) == part).astype(F32)
    blocks = [onehot[:, at : at + LANES] for at in range(0, count, LANES)]
    earlier = (iota((LANES, LANES), 0) < iota((LANES, LANES), 1)).astype(BF16)
    within = jnp.dot(
        jnp.concatenate(blocks, axis=0).astype(BF16), earlier, preferred_element_type=F32
    )
    offset = jnp.zeros((parts, 1), F32)
    pieces = []
    for index, piece in enumerate(blocks):
        before = within[index * parts : (index + 1) * parts, :] + offset
        pieces.append(jnp.sum(before * piece, axis=0, keepdims=True))
        offset = offset + jnp.sum(piece, axis=1, keepdims=True)
    position = jnp.concatenate(pieces, axis=1).astype(jnp.int32)
    counts = offset
    swapped = []
    for at in range(0, parts, 2 * mate):
        swapped += [counts[at + mate : at + 2 * mate], counts[at : at + mate]]
    free = (jnp.concatenate(swapped, axis=0) <= direct).astype(F32)
    crowded = jnp.max(jnp.where(counts > room, 1.0 - free, 0.0), axis=0, keepdims=True)
    mate_free = jnp.sum(onehot * free, axis=0, keepdims=True) > 0.5
    over = position - room
    other = jnp.bitwise_xor(part, mate) * room + direct + over
    target = jnp.where(over < 0, part * room + position, jnp.where(mate_free, other, -1))

    slot = dest_slot[...][None, :]
    power = jnp.right_shift(slot, 7)
    code = (slot - power * 128 + 128).astype(F32)
    for bit in POWERS:
        code = jnp.where(jnp.bitwise_and(power, bit) > 0, code * 2.0**bit, code)
    place_of = jnp.where(over < 0, position, room + direct - aligned + over)
    spot = (iota((LANES, count), 0) == place_of).astype(BF16)
    coded = lax.dot_general(
        (onehot * code).astype(BF16), spot, (((1,), (1,)), ((), ())), preferred_element_type=F32
    )
    coded = jnp.where(iota((parts, LANES), 1) == FLAG, crowded, coded)

    copies[0].wait()
    copies[1].wait()
    copies[4].wait()
    hidden = jnp.dot(features[...], w_first[...], preferred_element_type=F32)
    copies[5].wait()
    copies[6].wait()
    totals = []
    half_rows = count // 2
    for first in range(0, count, half_rows):
        piece = hidden[first : first + half_rows] + b_first[...].astype(F32)[None, :]
        piece = gelu(piece).astype(BF16)
        totals.append(jnp.dot(piece, w_second[...], preferred_element_type=F32))
    total = jnp.concatenate(totals, axis=0)
    embedded[...] = (total + b_second[...].astype(F32)[None, :]).astype(BF16)

    keep = pltpu.make_async_copy(embedded, embedded_out, leaving.at[parts // DESTS])
    keep.start()
    size = DESTS * room
    halves = width // LANES
    slot = iota((size, count), 0)
    leads = iota((DESTS, PIECE, LANES), 1) == 0
    sends = [keep]
    for group in range(parts // DESTS):
        select = (slot == target - group * size).astype(BF16)
        moved = jnp.dot(select, embedded[...], preferred_element_type=F32)
        dests = slice(group * DESTS, (group + 1) * DESTS)
        head, tail = [], []
        for half in range(halves):
            piece = moved[:, half * LANES : (half + 1) * LANES].reshape(DESTS, room, LANES)
            head.append(piece[:, :aligned])
            tail.append(piece[:, aligned:])
        codes = jnp.where(leads, coded[dests][:, None, :], 0.0)
        packed[dests] = jnp.concatenate(head + tail + [codes], axis=1).astype(BF16)
        sends.append(pltpu.make_async_copy(packed.at[dests], out.at[dests], leaving.at[group]))
        sends[-1].start()
    for send in sends:
        send.wait()


def project(
    parts, mate, sizes, features, w_first, b_first, w_second, b_second, part, slot
):
    rows, depth = features.shape
    hidden, width = w_second.shape
    length = (width // LANES) * sizes[0] + PIECE
    given = features, w_first, part, slot, b_first, w_second, b_second
    hbm = pl.BlockSpec(memory_space=pl.ANY)
    return pl.pallas_call(
        functools.partial(project_kernel, parts, mate, sizes),
        out_shape=[
            jax.ShapeDtypeStruct((parts, length, LANES), BF16),
            jax.ShapeDtypeStruct((rows, width), BF16),
        ],
        in_specs=[hbm] * len(given),
        out_specs=[hbm, hbm],
        scratch_shapes=[pltpu.VMEM(array.shape, array.dtype) for array in given]
        + [
            pltpu.VMEM((rows, width), BF16),
            pltpu.VMEM((parts, length, LANES), BF16),
            pltpu.SemaphoreType.DMA((len(given),)),
            pltpu.SemaphoreType.DMA((parts // DESTS + 1,)),
        ],
        compiler_params=pltpu.CompilerParams(vmem_limit_bytes=PROJECT_VMEM),
        cost_estimate=pl.CostEstimate(
            flops=2 * rows * hidden * (depth + width), bytes_accessed=8 << 20, transcendentals=0
        ),
        name="project",
    )(*given)


def arrived_rows(sizes, halves, arrived, extra):
    room, _, aligned = sizes
    beyond = room - aligned
    main = -(-2 * room // (3 * PIECE)) * PIECE
    parts = arrived.shape[0]
    found = ([], []), ([], [])
    lane = iota((GROUP, LANES), 1) // PIECE
    source = iota((GROUP, LANES), 0)
    for first in range(0, parts, GROUP):
        sources = slice(first, first + GROUP)
        got = arrived[sources].astype(F32)
        more = extra[sources].astype(F32)
        fields = []
        for half in range(halves):
            at = halves * aligned + half * beyond
            fields.append(
                jnp.concatenate(
                    [
                        got[:, half * aligned : (half + 1) * aligned],
                        got[:, at : at + beyond],
                        more[:, half * beyond : (half + 1) * beyond],
                    ],
                    axis=1,
                )
            )
        code = got[:, halves * room, :]
        power = jnp.zeros_like(code)
        for bit in POWERS:
            big = code >= 128.0 * 2.0**bit
            code = jnp.where(big, code * 2.0**-bit, code)
            power = jnp.where(big, power + bit, power)
        code = jnp.where(code >= 128.0, code + 128.0 * power - 128.0, -1.0)
        turned = pltpu.roll(code, 0, 1, stride=PIECE, stride_axis=0)
        for j in range((room + beyond) // PIECE):
            row = jnp.where(lane == lax.rem(source + j, GROUP), turned, 0.0)
            row = jnp.sum(row, axis=0, keepdims=True)
            row = pltpu.roll(row, (LANES - j * PIECE) % LANES, 1)
            rows = [
                field[:, j * PIECE : (j + 1) * PIECE, :].reshape(LANES, LANES) for field in fields
            ]
            ids, kept = found[0 if (j + 1) * PIECE <= main else 1]
            ids.append(row.astype(jnp.int32))
            kept.append(jnp.concatenate(rows, axis=1).astype(BF16))
    return [(jnp.concatenate(ids, axis=1), jnp.concatenate(rows, axis=0)) for ids, rows in found]


def fill(found, refs, blocks_of):
    for turn, (ids, rows) in enumerate(found):

        def write(turn=turn, ids=ids, rows=rows):
            for places, bases in blocks_of(refs[0]):
                block_rows = refs[0].shape[-2]
                slot = iota((block_rows, ids.shape[1]), 0)
                select = [(slot == ids - base * block_rows).astype(BF16) for base in bases]
                placed = jnp.dot(
                    jnp.concatenate(select, axis=0), rows, preferred_element_type=F32
                ).astype(BF16)
                for half, ref in enumerate(refs):
                    piece = placed[:, half * LANES : (half + 1) * LANES]
                    piece = piece.reshape(len(bases), block_rows, LANES)
                    ref[places] = piece if turn == 0 else ref[places] + piece

        if turn == 0:
            write()
        else:
            pl.when(jnp.max(ids) >= 0)(write)


def listed_kernel(sizes, halves, arrived, extra, halo_send, *sends):
    def blocks_of(send):
        for side in range(2):
            for first in range(0, send.shape[1], 4):
                bases = [halo_send[side, k] for k in range(first, first + 4)]
                yield (side, slice(first, first + 4)), bases

    fill(arrived_rows(sizes, halves, arrived, extra), sends, blocks_of)


def place_kernel(sizes, halves, arrived, extra, size, *starts):
    found = arrived_rows(sizes, halves, arrived, extra)
    size[0] = sum(jnp.sum((ids >= 0).astype(jnp.int32)) for ids, _ in found)

    def blocks_of(start):
        for first in range(0, start.shape[0], 4):
            yield slice(first, first + 4), range(first, first + 4)

    fill(found, starts, blocks_of)


def vmem_spec():
    return pl.BlockSpec(memory_space=pltpu.VMEM)


def smem_spec():
    return pl.BlockSpec(memory_space=pltpu.SMEM)


def listed_blocks(sizes, halves, block_rows, arrived, extra, halo_send):
    listed = halo_send.shape[1]
    depth = arrived.shape[0] * (2 * sizes[0] - sizes[2])
    return pl.pallas_call(
        functools.partial(listed_kernel, sizes, halves),
        out_shape=[jax.ShapeDtypeStruct((2, listed, block_rows, LANES), BF16)] * halves,
        in_specs=[vmem_spec(), vmem_spec(), smem_spec()],
        out_specs=[vmem_spec()] * halves,
        compiler_params=pltpu.CompilerParams(vmem_limit_bytes=VMEM_LIMIT),
        cost_estimate=pl.CostEstimate(
            flops=4 * listed * block_rows * depth * halves * LANES,
            bytes_accessed=4 << 20,
            transcendentals=0,
        ),
        name="listed",
    )(arrived, extra, halo_send)


def place(sizes, halves, block_count, block_rows, arrived, extra):
    depth = arrived.shape[0] * (2 * sizes[0] - sizes[2])
    return pl.pallas_call(
        functools.partial(place_kernel, sizes, halves),
        out_shape=[jax.ShapeDtypeStruct((1,), jnp.int32)]
        + [jax.ShapeDtypeStruct((block_count, block_rows, LANES), BF16)] * halves,
        in_specs=[vmem_spec()] * 2,
        out_specs=[smem_spec()] + [vmem_spec()] * halves,
        compiler_params=pltpu.CompilerParams(vmem_limit_bytes=VMEM_LIMIT),
        cost_estimate=pl.CostEstimate(
            flops=2 * block_count * block_rows * depth * halves * LANES,
            bytes_accessed=4 << 20,
            transcendentals=0,
        ),
        name="place",
    )(arrived, extra)


def inner_kernel(halo, tiles, coords, start, current, partial):
    block_count = start.shape[0]
    for b in range(block_count):
        term = jnp.dot(tiles[b], current[b], preferred_element_type=F32)
        partial[b] = (1.0 - ALPHA) * term + ALPHA * start[b].astype(F32)
    for t in range(block_count + 2 * halo, tiles.shape[0]):
        index = coords[2 * t + 1]
        source = current[jnp.minimum(index, block_count - 1)]
        source = jnp.where(index < block_count, source, jnp.zeros_like(source))
        term = jnp.dot(tiles[t], source, preferred_element_type=F32)
        partial[coords[2 * t]] += (1.0 - ALPHA) * term


def outer_kernel(half, *refs):
    tiles, coords, halo_send, size, partial, low, high = refs[:7]
    if half is None:
        out, send, terms, summed = refs[-4:]
    else:
        out, terms, summed, rounded, leaving = refs[-5:]
    block_count, block_rows, width = partial.shape
    listed = low.shape[0]
    own = block_count
    for t in range(own, tiles.shape[0]):
        if t < own + listed:
            source = low[t - own]
        elif t < own + 2 * listed:
            source = high[t - own - listed]
        else:
            index = coords[2 * t + 1]
            below = low[jnp.clip(index - own, 0, listed - 1)]
            above = high[jnp.clip(index - own - listed, 0, listed - 1)]
            source = jnp.where(index < own + listed, below, above)
            source = jnp.where(index < own, jnp.zeros_like(source), source)
        terms[t - own] = jnp.dot(tiles[t], source, preferred_element_type=F32)
    summed[...] = partial[...]
    for t in range(own, tiles.shape[0]):
        summed[coords[2 * t]] += (1.0 - ALPHA) * terms[t - own]
    row = iota((block_rows, width), 0)
    copies = []
    for b in range(block_count):
        mixed = jnp.where(row < size[0] - b * block_rows, summed[b], 0.0).astype(BF16)
        if half is None:
            out[b] = mixed
            continue
        rounded[b * block_rows : (b + 1) * block_rows, :] = mixed
        if (b + 1) % OUT_BLOCKS == 0:
            rows = slice((b + 1 - OUT_BLOCKS) * block_rows, (b + 1) * block_rows)
            columns = slice(half * width, (half + 1) * width)
            copies.append(
                pltpu.make_async_copy(
                    rounded.at[rows], out.at[rows, columns], leaving.at[len(copies)]
                )
            )
            copies[-1].start()
    for copy in copies:
        copy.wait()
    if half is None:
        for side in range(2):
            for k in range(listed):
                send[side, k] = out[halo_send[side, k]]


def inner(halo, tiles, coords, start, current):
    return pl.pallas_call(
        functools.partial(inner_kernel, halo),
        out_shape=jax.ShapeDtypeStruct(start.shape, F32),
        in_specs=[vmem_spec(), smem_spec(), vmem_spec(), vmem_spec()],
        out_specs=vmem_spec(),
        compiler_params=pltpu.CompilerParams(vmem_limit_bytes=VMEM_LIMIT),
        cost_estimate=pl.CostEstimate(
            flops=tiles.size * LANES, bytes_accessed=4 << 20, transcendentals=0
        ),
        name="inner",
    )(tiles, coords, start, current)


def outer(tiles, coords, halo_send, size, partial, low, high, half=None, halves=1, held=None):
    block_count, block_rows, width = partial.shape
    listed = low.shape[0]
    operands = [tiles, coords, halo_send, size, partial, low, high]
    vmem = vmem_spec()
    in_specs = [vmem, smem_spec(), smem_spec(), smem_spec(), vmem, vmem, vmem]
    scratch = [
        pltpu.VMEM((tiles.shape[0] - block_count, block_rows, width), F32),
        pltpu.VMEM((block_count, block_rows, width), F32),
    ]
    aliases = {}
    if half is None:
        out_shape = [
            jax.ShapeDtypeStruct((block_count, block_rows, width), BF16),
            jax.ShapeDtypeStruct((2, listed, block_rows, width), BF16),
        ]
        out_specs = [vmem, vmem]
    else:
        capacity = block_count * block_rows
        out_shape = jax.ShapeDtypeStruct((capacity, width * halves), BF16)
        out_specs = pl.BlockSpec(memory_space=pl.ANY)
        scratch += [
            pltpu.VMEM((capacity, width), BF16),
            pltpu.SemaphoreType.DMA((block_count // OUT_BLOCKS,)),
        ]
        if held is not None:
            aliases = {len(operands): 0}
            operands.append(held)
            in_specs.append(pl.BlockSpec(memory_space=pl.ANY))
    return pl.pallas_call(
        functools.partial(outer_kernel, half),
        out_shape=out_shape,
        in_specs=in_specs,
        out_specs=out_specs,
        scratch_shapes=scratch,
        input_output_aliases=aliases,
        compiler_params=pltpu.CompilerParams(vmem_limit_bytes=VMEM_LIMIT),
        cost_estimate=pl.CostEstimate(
            flops=tiles.size * width, bytes_accessed=4 << 20, transcendentals=0
        ),
        name="outer",
    )(*operands)


def all_to_all(payload):
    return lax.all_to_all(payload, ("dp", "dom"), split_axis=0, concat_axis=0, tiled=True)


def late_rows(parts, sizes, embedded, dest_part):
    room, direct, aligned = sizes
    shared = room - aligned
    count, width = embedded.shape
    onehot = (dest_part[:, None] == jnp.arange(parts, dtype=jnp.int32)[None, :]).astype(BF16)
    row = jnp.arange(count, dtype=jnp.int32)
    earlier = (row[None, :] < row[:, None]).astype(BF16)
    before = jnp.dot(earlier, onehot, preferred_element_type=F32)
    position = jnp.sum(before * onehot.astype(F32), axis=1).astype(jnp.int32)
    over = position - room
    target = jnp.where(over < 0, -1, dest_part * shared + direct - aligned + over)
    select = (jnp.arange(parts * shared, dtype=jnp.int32)[:, None] == target[None, :]).astype(BF16)
    moved = jnp.dot(select, embedded, preferred_element_type=F32).astype(BF16)
    moved = moved.reshape(parts, shared, width // LANES, LANES)
    return jnp.swapaxes(moved, 1, 2).reshape(parts, width // LANES * shared, LANES)


def local(
    features,
    w_first,
    b_first,
    w_second,
    b_second,
    dest_part,
    dest_slot,
    tile_coords,
    tile_values,
    halo_send,
):
    count_dp = lax.axis_size("dp")
    count_dom = lax.axis_size("dom")
    parts = count_dp * count_dom
    row_count = features.shape[0]
    capacity = 3 * row_count
    most = -(-capacity // parts)
    room = -(-3 * most // 32) * 8
    direct = 2 * room - most
    sizes = room, direct, min(direct // 8 * 8, room - 8)
    width = w_second.shape[1]
    halves = width // LANES
    block_rows = tile_values.shape[1]
    block_count = capacity // block_rows
    outgoing, embedded = project(
        parts,
        count_dom,
        sizes,
        features,
        w_first,
        b_first,
        w_second,
        b_second,
        dest_part,
        dest_slot,
    )
    arrived = all_to_all(outgoing)
    crowded = jnp.any(arrived[:, halves * room, FLAG] > 0.5)
    from_mate = lax.ppermute(
        arrived[:, halves * sizes[2] : halves * room, :],
        "dp",
        [(i, i ^ 1) for i in range(count_dp)],
    )
    extra = lax.cond(
        crowded,
        lambda: all_to_all(late_rows(parts, sizes, embedded, dest_part)),
        lambda: from_mate,
    )
    coords = tile_coords.reshape(-1)
    lists = halo_send[0]
    forward = [(i, (i + 1) % count_dom) for i in range(count_dom)]
    backward = [((i + 1) % count_dom, i) for i in range(count_dom)]

    def exchange(send):
        return lax.ppermute(send[0], "dom", forward), lax.ppermute(send[1], "dom", backward)

    halos = [
        exchange(send) for send in listed_blocks(sizes, halves, block_rows, arrived, extra, lists)
    ]
    size, *starts = place(sizes, halves, block_count, block_rows, arrived, extra)
    fields = list(starts)
    held = None
    for repeat in range(HOPS):
        for half in range(halves):
            partial = inner(lists.shape[1], tile_values, coords, starts[half], fields[half])
            operands = tile_values, coords, lists, size, partial, *halos[half]
            if repeat < HOPS - 1:
                fields[half], send = outer(*operands)
                halos[half] = exchange(send)
            else:
                held = outer(*operands, half=half, halves=halves, held=held)
    return held


def solution(mesh):
    placed = (
        P(("dp", "dom"), None),
        P(),
        P(),
        P(),
        P(),
        P(("dp", "dom")),
        P(("dp", "dom")),
        P(("dp", "dom"), None),
        P(("dp", "dom"), None, None),
        P(("dp", "dom"), None, None),
    )
    return jax.shard_map(
        local, mesh=mesh, in_specs=placed, out_specs=P(("dp", "dom"), None), check_vma=False
    )
```

```python
import functools

import jax
import jax.numpy as jnp
from jax import lax
from jax.experimental import pallas as pl
from jax.experimental.pallas import tpu as pltpu
from jax.sharding import PartitionSpec as P

HOPS = 2
ALPHA = 0.1
LANES = 128
PIECE = 8
GROUP = LANES // PIECE
DESTS = 8
FLAG = LANES - 1
POWERS = 16, 8, 4, 2, 1
OUT_BLOCKS = 6
VMEM_LIMIT = 48 * 1024 * 1024
PROJECT_VMEM = 62 * 1024 * 1024

BF16 = jnp.bfloat16
F32 = jnp.float32


def iota(shape, dim):
    return lax.broadcasted_iota(jnp.int32, shape, dim)


def gelu(value):
    return 0.5 * value * (1.0 + lax.erf(value * (0.5**0.5)))


def project_kernel(parts, mate, sizes, *refs):
    given, (out, embedded_out) = refs[:7], refs[7:9]
    held = refs[9:16]
    features, w_first, dest_part, dest_slot, b_first, w_second, b_second = held
    embedded, packed, arrival, leaving = refs[16:]
    room, direct, aligned = sizes
    copies = [
        pltpu.make_async_copy(source, kept, arrival.at[index])
        for index, (source, kept) in enumerate(zip(given, held))
    ]
    for index in (2, 3, 0, 1, 4, 5, 6):
        copies[index].start()
    copies[2].wait()
    copies[3].wait()
    width = w_second.shape[1]
    count = dest_part.shape[0]
    part = dest_part[...][None, :]
    onehot = (iota((parts, count), 0) == part).astype(F32)
    blocks = [onehot[:, at : at + LANES] for at in range(0, count, LANES)]
    earlier = (iota((LANES, LANES), 0) < iota((LANES, LANES), 1)).astype(BF16)
    within = jnp.dot(
        jnp.concatenate(blocks, axis=0).astype(BF16), earlier, preferred_element_type=F32
    )
    offset = jnp.zeros((parts, 1), F32)
    pieces = []
    for index, piece in enumerate(blocks):
        before = within[index * parts : (index + 1) * parts, :] + offset
        pieces.append(jnp.sum(before * piece, axis=0, keepdims=True))
        offset = offset + jnp.sum(piece, axis=1, keepdims=True)
    position = jnp.concatenate(pieces, axis=1).astype(jnp.int32)
    counts = offset
    swapped = []
    for at in range(0, parts, 2 * mate):
        swapped += [counts[at + mate : at + 2 * mate], counts[at : at + mate]]
    free = (jnp.concatenate(swapped, axis=0) <= direct).astype(F32)
    crowded = jnp.max(jnp.where(counts > room, 1.0 - free, 0.0), axis=0, keepdims=True)
    mate_free = jnp.sum(onehot * free, axis=0, keepdims=True) > 0.5
    over = position - room
    other = jnp.bitwise_xor(part, mate) * room + direct + over
    target = jnp.where(over < 0, part * room + position, jnp.where(mate_free, other, -1))

    slot = dest_slot[...][None, :]
    power = jnp.right_shift(slot, 7)
    code = (slot - power * 128 + 128).astype(F32)
    for bit in POWERS:
        code = jnp.where(jnp.bitwise_and(power, bit) > 0, code * 2.0**bit, code)
    place_of = jnp.where(over < 0, position, room + direct - aligned + over)
    spot = (iota((LANES, count), 0) == place_of).astype(BF16)
    coded = lax.dot_general(
        (onehot * code).astype(BF16), spot, (((1,), (1,)), ((), ())), preferred_element_type=F32
    )
    coded = jnp.where(iota((parts, LANES), 1) == FLAG, crowded, coded)

    copies[0].wait()
    copies[1].wait()
    copies[4].wait()
    hidden = jnp.dot(features[...], w_first[...], preferred_element_type=F32)
    copies[5].wait()
    copies[6].wait()
    totals = []
    half_rows = count // 2
    for first in range(0, count, half_rows):
        piece = hidden[first : first + half_rows] + b_first[...].astype(F32)[None, :]
        piece = gelu(piece).astype(BF16)
        totals.append(jnp.dot(piece, w_second[...], preferred_element_type=F32))
    total = jnp.concatenate(totals, axis=0)
    embedded[...] = (total + b_second[...].astype(F32)[None, :]).astype(BF16)

    keep = pltpu.make_async_copy(embedded, embedded_out, leaving.at[parts // DESTS])
    keep.start()
    size = DESTS * room
    halves = width // LANES
    slot = iota((size, count), 0)
    leads = iota((DESTS, PIECE, LANES), 1) == 0
    sends = [keep]
    for group in range(parts // DESTS):
        select = (slot == target - group * size).astype(BF16)
        moved = jnp.dot(select, embedded[...], preferred_element_type=F32)
        dests = slice(group * DESTS, (group + 1) * DESTS)
        head, tail = [], []
        for half in range(halves):
            piece = moved[:, half * LANES : (half + 1) * LANES].reshape(DESTS, room, LANES)
            head.append(piece[:, :aligned])
            tail.append(piece[:, aligned:])
        codes = jnp.where(leads, coded[dests][:, None, :], 0.0)
        packed[dests] = jnp.concatenate(head + tail + [codes], axis=1).astype(BF16)
        sends.append(pltpu.make_async_copy(packed.at[dests], out.at[dests], leaving.at[group]))
        sends[-1].start()
    for send in sends:
        send.wait()


def project(
    parts, mate, sizes, features, w_first, b_first, w_second, b_second, part, slot
):
    rows, depth = features.shape
    hidden, width = w_second.shape
    length = (width // LANES) * sizes[0] + PIECE
    given = features, w_first, part, slot, b_first, w_second, b_second
    hbm = pl.BlockSpec(memory_space=pl.ANY)
    return pl.pallas_call(
        functools.partial(project_kernel, parts, mate, sizes),
        out_shape=[
            jax.ShapeDtypeStruct((parts, length, LANES), BF16),
            jax.ShapeDtypeStruct((rows, width), BF16),
        ],
        in_specs=[hbm] * len(given),
        out_specs=[hbm, hbm],
        scratch_shapes=[pltpu.VMEM(array.shape, array.dtype) for array in given]
        + [
            pltpu.VMEM((rows, width), BF16),
            pltpu.VMEM((parts, length, LANES), BF16),
            pltpu.SemaphoreType.DMA((len(given),)),
            pltpu.SemaphoreType.DMA((parts // DESTS + 1,)),
        ],
        compiler_params=pltpu.CompilerParams(vmem_limit_bytes=PROJECT_VMEM),
        cost_estimate=pl.CostEstimate(
            flops=2 * rows * hidden * (depth + width), bytes_accessed=8 << 20, transcendentals=0
        ),
        name="project",
    )(*given)


def arrived_rows(sizes, halves, arrived, extra):
    room, _, aligned = sizes
    beyond = room - aligned
    main = -(-2 * room // (3 * PIECE)) * PIECE
    parts = arrived.shape[0]
    found = ([], []), ([], [])
    lane = iota((GROUP, LANES), 1) // PIECE
    source = iota((GROUP, LANES), 0)
    for first in range(0, parts, GROUP):
        sources = slice(first, first + GROUP)
        got = arrived[sources].astype(F32)
        more = extra[sources].astype(F32)
        fields = []
        for half in range(halves):
            at = halves * aligned + half * beyond
            fields.append(
                jnp.concatenate(
                    [
                        got[:, half * aligned : (half + 1) * aligned],
                        got[:, at : at + beyond],
                        more[:, half * beyond : (half + 1) * beyond],
                    ],
                    axis=1,
                )
            )
        code = got[:, halves * room, :]
        power = jnp.zeros_like(code)
        for bit in POWERS:
            big = code >= 128.0 * 2.0**bit
            code = jnp.where(big, code * 2.0**-bit, code)
            power = jnp.where(big, power + bit, power)
        code = jnp.where(code >= 128.0, code + 128.0 * power - 128.0, -1.0)
        turned = pltpu.roll(code, 0, 1, stride=PIECE, stride_axis=0)
        for j in range((room + beyond) // PIECE):
            row = jnp.where(lane == lax.rem(source + j, GROUP), turned, 0.0)
            row = jnp.sum(row, axis=0, keepdims=True)
            row = pltpu.roll(row, (LANES - j * PIECE) % LANES, 1)
            rows = [
                field[:, j * PIECE : (j + 1) * PIECE, :].reshape(LANES, LANES) for field in fields
            ]
            ids, kept = found[0 if (j + 1) * PIECE <= main else 1]
            ids.append(row.astype(jnp.int32))
            kept.append(jnp.concatenate(rows, axis=1).astype(BF16))
    return [(jnp.concatenate(ids, axis=1), jnp.concatenate(rows, axis=0)) for ids, rows in found]


def fill(found, refs, blocks_of):
    for turn, (ids, rows) in enumerate(found):

        def write(turn=turn, ids=ids, rows=rows):
            for places, bases in blocks_of(refs[0]):
                block_rows = refs[0].shape[-2]
                slot = iota((block_rows, ids.shape[1]), 0)
                select = [(slot == ids - base * block_rows).astype(BF16) for base in bases]
                placed = jnp.dot(
                    jnp.concatenate(select, axis=0), rows, preferred_element_type=F32
                ).astype(BF16)
                for half, ref in enumerate(refs):
                    piece = placed[:, half * LANES : (half + 1) * LANES]
                    piece = piece.reshape(len(bases), block_rows, LANES)
                    ref[places] = piece if turn == 0 else ref[places] + piece

        if turn == 0:
            write()
        else:
            pl.when(jnp.max(ids) >= 0)(write)


def listed_kernel(sizes, halves, arrived, extra, halo_send, *sends):
    def blocks_of(send):
        for side in range(2):
            for first in range(0, send.shape[1], 4):
                bases = [halo_send[side, k] for k in range(first, first + 4)]
                yield (side, slice(first, first + 4)), bases

    fill(arrived_rows(sizes, halves, arrived, extra), sends, blocks_of)


def place_kernel(sizes, halves, arrived, extra, size, *starts):
    found = arrived_rows(sizes, halves, arrived, extra)
    size[0] = sum(jnp.sum((ids >= 0).astype(jnp.int32)) for ids, _ in found)

    def blocks_of(start):
        for first in range(0, start.shape[0], 4):
            yield slice(first, first + 4), range(first, first + 4)

    fill(found, starts, blocks_of)


def vmem_spec():
    return pl.BlockSpec(memory_space=pltpu.VMEM)


def smem_spec():
    return pl.BlockSpec(memory_space=pltpu.SMEM)


def listed_blocks(sizes, halves, block_rows, arrived, extra, halo_send):
    listed = halo_send.shape[1]
    depth = arrived.shape[0] * (2 * sizes[0] - sizes[2])
    return pl.pallas_call(
        functools.partial(listed_kernel, sizes, halves),
        out_shape=[jax.ShapeDtypeStruct((2, listed, block_rows, LANES), BF16)] * halves,
        in_specs=[vmem_spec(), vmem_spec(), smem_spec()],
        out_specs=[vmem_spec()] * halves,
        compiler_params=pltpu.CompilerParams(vmem_limit_bytes=VMEM_LIMIT),
        cost_estimate=pl.CostEstimate(
            flops=4 * listed * block_rows * depth * halves * LANES,
            bytes_accessed=4 << 20,
            transcendentals=0,
        ),
        name="listed",
    )(arrived, extra, halo_send)


def place(sizes, halves, block_count, block_rows, arrived, extra):
    depth = arrived.shape[0] * (2 * sizes[0] - sizes[2])
    return pl.pallas_call(
        functools.partial(place_kernel, sizes, halves),
        out_shape=[jax.ShapeDtypeStruct((1,), jnp.int32)]
        + [jax.ShapeDtypeStruct((block_count, block_rows, LANES), BF16)] * halves,
        in_specs=[vmem_spec()] * 2,
        out_specs=[smem_spec()] + [vmem_spec()] * halves,
        compiler_params=pltpu.CompilerParams(vmem_limit_bytes=VMEM_LIMIT),
        cost_estimate=pl.CostEstimate(
            flops=2 * block_count * block_rows * depth * halves * LANES,
            bytes_accessed=4 << 20,
            transcendentals=0,
        ),
        name="place",
    )(arrived, extra)


def inner_kernel(halo, tiles, coords, start, current, partial):
    block_count = start.shape[0]
    for b in range(block_count):
        term = jnp.dot(tiles[b], current[b], preferred_element_type=F32)
        partial[b] = (1.0 - ALPHA) * term + ALPHA * start[b].astype(F32)
    for t in range(block_count + 2 * halo, tiles.shape[0]):
        index = coords[1, t]
        source = current[jnp.minimum(index, block_count - 1)]
        source = jnp.where(index < block_count, source, jnp.zeros_like(source))
        term = jnp.dot(tiles[t], source, preferred_element_type=F32)
        partial[coords[0, t]] += (1.0 - ALPHA) * term


def outer_kernel(half, *refs):
    tiles, coords, halo_send, size, partial, low, high = refs[:7]
    if half is None:
        out, send, terms, summed = refs[-4:]
    else:
        out, terms, summed, rounded, leaving = refs[-5:]
    block_count, block_rows, width = partial.shape
    listed = low.shape[0]
    own = block_count
    for t in range(own, tiles.shape[0]):
        if t < own + listed:
            source = low[t - own]
        elif t < own + 2 * listed:
            source = high[t - own - listed]
        else:
            index = coords[1, t]
            below = low[jnp.clip(index - own, 0, listed - 1)]
            above = high[jnp.clip(index - own - listed, 0, listed - 1)]
            source = jnp.where(index < own + listed, below, above)
            source = jnp.where(index < own, jnp.zeros_like(source), source)
        terms[t - own] = jnp.dot(tiles[t], source, preferred_element_type=F32)
    summed[...] = partial[...]
    for t in range(own, tiles.shape[0]):
        summed[coords[0, t]] += (1.0 - ALPHA) * terms[t - own]
    row = iota((block_rows, width), 0)
    copies = []
    for b in range(block_count):
        mixed = jnp.where(row < size[0] - b * block_rows, summed[b], 0.0).astype(BF16)
        if half is None:
            out[b] = mixed
            continue
        rounded[b * block_rows : (b + 1) * block_rows, :] = mixed
        if (b + 1) % OUT_BLOCKS == 0:
            rows = slice((b + 1 - OUT_BLOCKS) * block_rows, (b + 1) * block_rows)
            columns = slice(half * width, (half + 1) * width)
            copies.append(
                pltpu.make_async_copy(
                    rounded.at[rows], out.at[rows, columns], leaving.at[len(copies)]
                )
            )
            copies[-1].start()
    for copy in copies:
        copy.wait()
    if half is None:
        for side in range(2):
            for k in range(listed):
                send[side, k] = out[halo_send[side, k]]


def inner(halo, tiles, coords, start, current):
    return pl.pallas_call(
        functools.partial(inner_kernel, halo),
        out_shape=jax.ShapeDtypeStruct(start.shape, F32),
        in_specs=[vmem_spec(), smem_spec(), vmem_spec(), vmem_spec()],
        out_specs=vmem_spec(),
        compiler_params=pltpu.CompilerParams(vmem_limit_bytes=VMEM_LIMIT),
        cost_estimate=pl.CostEstimate(
            flops=tiles.size * LANES, bytes_accessed=4 << 20, transcendentals=0
        ),
        name="inner",
    )(tiles, coords, start, current)


def outer(tiles, coords, halo_send, size, partial, low, high, half=None, halves=1, held=None):
    block_count, block_rows, width = partial.shape
    listed = low.shape[0]
    operands = [tiles, coords, halo_send, size, partial, low, high]
    vmem = vmem_spec()
    in_specs = [vmem, smem_spec(), smem_spec(), smem_spec(), vmem, vmem, vmem]
    scratch = [
        pltpu.VMEM((tiles.shape[0] - block_count, block_rows, width), F32),
        pltpu.VMEM((block_count, block_rows, width), F32),
    ]
    aliases = {}
    if half is None:
        out_shape = [
            jax.ShapeDtypeStruct((block_count, block_rows, width), BF16),
            jax.ShapeDtypeStruct((2, listed, block_rows, width), BF16),
        ]
        out_specs = [vmem, vmem]
    else:
        capacity = block_count * block_rows
        out_shape = jax.ShapeDtypeStruct((capacity, width * halves), BF16)
        out_specs = pl.BlockSpec(memory_space=pl.ANY)
        scratch += [
            pltpu.VMEM((capacity, width), BF16),
            pltpu.SemaphoreType.DMA((block_count // OUT_BLOCKS,)),
        ]
        if held is not None:
            aliases = {len(operands): 0}
            operands.append(held)
            in_specs.append(pl.BlockSpec(memory_space=pl.ANY))
    return pl.pallas_call(
        functools.partial(outer_kernel, half),
        out_shape=out_shape,
        in_specs=in_specs,
        out_specs=out_specs,
        scratch_shapes=scratch,
        input_output_aliases=aliases,
        compiler_params=pltpu.CompilerParams(vmem_limit_bytes=VMEM_LIMIT),
        cost_estimate=pl.CostEstimate(
            flops=tiles.size * width, bytes_accessed=4 << 20, transcendentals=0
        ),
        name="outer",
    )(*operands)


def all_to_all(payload):
    return lax.all_to_all(payload, ("dp", "dom"), split_axis=0, concat_axis=0, tiled=True)


def late_rows(parts, sizes, embedded, dest_part):
    room, direct, aligned = sizes
    shared = room - aligned
    count, width = embedded.shape
    onehot = (dest_part[:, None] == jnp.arange(parts, dtype=jnp.int32)[None, :]).astype(BF16)
    row = jnp.arange(count, dtype=jnp.int32)
    earlier = (row[None, :] < row[:, None]).astype(BF16)
    before = jnp.dot(earlier, onehot, preferred_element_type=F32)
    position = jnp.sum(before * onehot.astype(F32), axis=1).astype(jnp.int32)
    over = position - room
    target = jnp.where(over < 0, -1, dest_part * shared + direct - aligned + over)
    select = (jnp.arange(parts * shared, dtype=jnp.int32)[:, None] == target[None, :]).astype(BF16)
    moved = jnp.dot(select, embedded, preferred_element_type=F32).astype(BF16)
    moved = moved.reshape(parts, shared, width // LANES, LANES)
    return jnp.swapaxes(moved, 1, 2).reshape(parts, width // LANES * shared, LANES)


def local(
    features,
    w_first,
    b_first,
    w_second,
    b_second,
    dest_part,
    dest_slot,
    tile_coords,
    tile_values,
    halo_send,
):
    count_dp = lax.axis_size("dp")
    count_dom = lax.axis_size("dom")
    parts = count_dp * count_dom
    row_count = features.shape[0]
    capacity = 3 * row_count
    most = -(-capacity // parts)
    room = -(-3 * most // 32) * 8
    direct = 2 * room - most
    sizes = room, direct, min(direct // 8 * 8, room - 8)
    width = w_second.shape[1]
    halves = width // LANES
    block_rows = tile_values.shape[1]
    block_count = capacity // block_rows
    outgoing, embedded = project(
        parts,
        count_dom,
        sizes,
        features,
        w_first,
        b_first,
        w_second,
        b_second,
        dest_part,
        dest_slot,
    )
    arrived = all_to_all(outgoing)
    crowded = jnp.any(arrived[:, halves * room, FLAG] > 0.5)
    from_mate = lax.ppermute(
        arrived[:, halves * sizes[2] : halves * room, :],
        "dp",
        [(i, i ^ 1) for i in range(count_dp)],
    )
    extra = lax.cond(
        crowded,
        lambda: all_to_all(late_rows(parts, sizes, embedded, dest_part)),
        lambda: from_mate,
    )
    coords = tile_coords.T
    lists = halo_send[0]
    forward = [(i, (i + 1) % count_dom) for i in range(count_dom)]
    backward = [((i + 1) % count_dom, i) for i in range(count_dom)]

    def exchange(send):
        return lax.ppermute(send[0], "dom", forward), lax.ppermute(send[1], "dom", backward)

    halos = [
        exchange(send) for send in listed_blocks(sizes, halves, block_rows, arrived, extra, lists)
    ]
    size, *starts = place(sizes, halves, block_count, block_rows, arrived, extra)
    fields = list(starts)
    held = None
    for repeat in range(HOPS):
        for half in range(halves):
            partial = inner(lists.shape[1], tile_values, coords, starts[half], fields[half])
            operands = tile_values, coords, lists, size, partial, *halos[half]
            if repeat < HOPS - 1:
                fields[half], send = outer(*operands)
                halos[half] = exchange(send)
            else:
                held = outer(*operands, half=half, halves=halves, held=held)
    return held


def solution(mesh):
    placed = (
        P(("dp", "dom"), None),
        P(),
        P(),
        P(),
        P(),
        P(("dp", "dom")),
        P(("dp", "dom")),
        P(("dp", "dom"), None),
        P(("dp", "dom"), None, None),
        P(("dp", "dom"), None, None),
    )
    return jax.shard_map(
        local, mesh=mesh, in_specs=placed, out_specs=P(("dp", "dom"), None), check_vma=False
    )
```
